128 devices in a mesh: wide: 16 (over y, z_hi, core), narrow: 8 (over x, z_lo).
Axes of the slice: x: 4, y: 4, z: 4 (z_hi: 2, z_lo: 2; z = z_hi * 2 + z_lo), core: 2. Of those that a mesh axis runs over, the one named last changes fastest.
Arguments:
- node_hidden_state: bfloat16 [262144, 128], P(('wide', 'narrow')), may hold values from -6 to 6
- edge_hidden_state: bfloat16 [1572864, 128], P(('wide', 'narrow')), may hold values from -6 to 6
- node_output_gradient: bfloat16 [262144, 128], P(('wide', 'narrow')), may hold values from -6 to 6
- edge_output_gradient: bfloat16 [1572864, 128], P(('wide', 'narrow')), may hold values from -6 to 6
- senders: int32 [1572864], P(('wide', 'narrow')), may hold values from 0 to 4095
- receivers: int32 [1572864], P(('wide', 'narrow')), may hold values from 0 to 2047, as said below
- edge_slot_count: int32 [128], P(('wide', 'narrow')), may hold values from 3072 to 12288, as said below
- outbound_rows: int32 [128, 4, 512], P(('wide', 'narrow')), may hold values from 0 to 2047, as said below
- edge_weight_in: bfloat16 [384, 128], replicated, may hold values from -0.3125 to 0.3125
- edge_weight_mid: bfloat16 [128, 128], replicated, may hold values from -0.5 to 0.5
- edge_weight_out: bfloat16 [128, 128], replicated, may hold values from -0.5 to 0.5
- node_weight_in: bfloat16 [256, 128], replicated, may hold values from -0.375 to 0.375
- node_weight_mid: bfloat16 [128, 128], replicated, may hold values from -0.5 to 0.5
- node_weight_out: bfloat16 [128, 128], replicated, may hold values from -0.5 to 0.5
Outputs:
- node_state_gradient: float32 [262144, 128], P(('wide', 'narrow'))
- edge_grad: bfloat16 [1572864, 128], P(('wide', 'narrow'))
- edge_in_grad: float32 [384, 128], replicated
- edge_mid_grad: float32 [128, 128], replicated
- edge_out_grad: float32 [128, 128], replicated
- node_in_grad: float32 [256, 128], replicated
- node_mid_grad: float32 [128, 128], replicated
- node_out_grad: float32 [128, 128], replicated
The draws below stay inside these ranges and needn't reach their ends.
Inputs may be any that keep to these rules, and one draw needn't show every extreme that they name: `receivers`: Non-decreasing within each partition's 12288 slots. `edge_slot_count`: some partition is full in every draw. `outbound_rows`: the 512 rows of one list are distinct.
All inputs are finite; a program needn't handle non-finite values.
Results may differ from the reference program's by a relative error of at most 0.015.
Values may be sent and summed in bfloat16 or wider, within the bound.
A program may use at most 128 MiB of HBM per device.

```python
import math
from functools import partial
import jax
import jax.numpy as jnp
from jax import lax

LATENT_WIDTH = 128
PART_NODE_COUNT = 2048
BORDER_NODES = 512
PART_EDGE_SLOTS = 12288
GRAPH_PIECES = 128
NODES = 262144
EDGES = 1572864
N_WIDE = 16
N_NARROW = 8


def partition_counts(key):
    opening_key, middle_key, closing_key = jax.random.split(jax.random.fold_in(key, 7), 3)
    baseline_count = PART_EDGE_SLOTS // 4 + jax.random.randint(opening_key, (GRAPH_PIECES,), 0, PART_EDGE_SLOTS // 4 + 1)
    complete_mask = jax.random.randint(middle_key, (GRAPH_PIECES,), 0, 8) == 0
    picked_entries = jax.random.randint(closing_key, (), 0, GRAPH_PIECES)
    complete_mask = jnp.logical_or(complete_mask, jnp.arange(GRAPH_PIECES) == picked_entries)
    return jnp.where(complete_mask, PART_EDGE_SLOTS, baseline_count).astype(jnp.int32)


def draw_edge_slot_count(key, part):
    return partition_counts(key)


def draw_receivers(key, part):
    counts = partition_counts(key)
    unsorted_index = jax.random.randint(jax.random.fold_in(key, 13), (GRAPH_PIECES, PART_EDGE_SLOTS), 0, PART_NODE_COUNT)
    live_mask = jnp.arange(PART_EDGE_SLOTS)[None, :] < counts[:, None]
    unsorted_index = jnp.where(live_mask, unsorted_index, PART_NODE_COUNT - 1)
    return jnp.sort(unsorted_index, axis=1).reshape(EDGES).astype(jnp.int32)


def draw_senders(key, part):
    opening_key, middle_key, closing_key = jax.random.split(jax.random.fold_in(key, 17), 3)
    border_direction = jax.random.randint(opening_key, (GRAPH_PIECES, PART_EDGE_SLOTS), 0, 4) == 0
    local_index = jax.random.randint(middle_key, (GRAPH_PIECES, PART_EDGE_SLOTS), 0, PART_NODE_COUNT)
    remote_index = PART_NODE_COUNT + jax.random.randint(closing_key, (GRAPH_PIECES, PART_EDGE_SLOTS), 0, 4 * BORDER_NODES)
    chosen_ids = jnp.where(border_direction, remote_index, local_index)
    chosen_ids = chosen_ids.at[:, 1].set(PART_NODE_COUNT + 4 * BORDER_NODES - 1)
    return chosen_ids.reshape(EDGES).astype(jnp.int32)


def draw_outbound_rows(key, part):
    send_list_keys = jax.random.split(jax.random.fold_in(key, 19), GRAPH_PIECES * 4)

    def single_send_list(list_key):
        return jax.random.permutation(list_key, PART_NODE_COUNT)[:BORDER_NODES]
    return jax.vmap(single_send_list)(send_list_keys).reshape(GRAPH_PIECES, 4, BORDER_NODES).astype(jnp.int32)


def level_of(stream_key, shape, shards, least, high):
    def one(dim, shards_of):
        draws = jax.random.uniform(jax.random.fold_in(jax.random.fold_in(stream_key, 6), dim), (shards_of,), jnp.float32, least / len(shards), high / len(shards))
        return jnp.repeat(jnp.exp(draws), shape[dim] // shards_of).reshape((-1,) + (1,) * (len(shape) - dim - 1))

    gain = one(*shards[0])
    for cut in shards[1:]:
        gain = gain * one(*cut)
    return gain


def noise(rng, extent, spread, reach, cuts=(), held_as=jnp.bfloat16):
    loudness = level_of(rng, extent, cuts, -0.22, 0.18) if cuts else 1.0
    drawn = jax.random.normal(rng, extent, jnp.float32) * spread * loudness
    return jnp.minimum(jnp.maximum(drawn, -reach), reach).astype(held_as)


def setup_inputs(seed: int = 0) -> dict:
    arg_keys = jax.random.split(jax.random.key(seed), 15)
    return {
        "node_hidden_state": noise(arg_keys[0], (NODES, LATENT_WIDTH), 1.0, 6.0, ((0, 128),)),
        "edge_hidden_state": noise(arg_keys[1], (EDGES, LATENT_WIDTH), 1.0, 6.0, ((0, 128),)),
        "node_output_gradient": noise(arg_keys[2], (NODES, LATENT_WIDTH), 1.0, 6.0, ((0, 128),)),
        "edge_output_gradient": noise(arg_keys[3], (EDGES, LATENT_WIDTH), 1.0, 6.0, ((0, 128),)),
        "senders": draw_senders(jax.random.fold_in(arg_keys[14], 71), 0),
        "receivers": draw_receivers(jax.random.fold_in(arg_keys[14], 71), 0),
        "edge_slot_count": draw_edge_slot_count(jax.random.fold_in(arg_keys[14], 71), 0),
        "outbound_rows": draw_outbound_rows(jax.random.fold_in(arg_keys[14], 71), 0),
        "edge_weight_in": noise(arg_keys[8], (3 * LATENT_WIDTH, LATENT_WIDTH), (3 * LATENT_WIDTH) ** -0.5, 0.3125),
        "edge_weight_mid": noise(arg_keys[9], (LATENT_WIDTH, LATENT_WIDTH), LATENT_WIDTH ** -0.5, 0.5),
        "edge_weight_out": noise(arg_keys[10], (LATENT_WIDTH, LATENT_WIDTH), LATENT_WIDTH ** -0.5, 0.5),
        "node_weight_in": noise(arg_keys[11], (2 * LATENT_WIDTH, LATENT_WIDTH), (2 * LATENT_WIDTH) ** -0.5, 0.375),
        "node_weight_mid": noise(arg_keys[12], (LATENT_WIDTH, LATENT_WIDTH), LATENT_WIDTH ** -0.5, 0.5),
        "node_weight_out": noise(arg_keys[13], (LATENT_WIDTH, LATENT_WIDTH), LATENT_WIDTH ** -0.5, 0.5),
    }


epsilon = 1e-05

def silu_slope(values):
    sigmoid = jax.nn.sigmoid(values)
    return sigmoid * (1.0 + values * (1.0 - sigmoid))

def mlp_forward(inputs, weight_in, weight_mid, weight_out):
    first_pre = jnp.dot(inputs, weight_in, preferred_element_type=jnp.float32)
    first_act = jax.nn.silu(first_pre).astype(jnp.bfloat16)
    second_pre = jnp.dot(first_act, weight_mid, preferred_element_type=jnp.float32)
    second_act = jax.nn.silu(second_pre).astype(jnp.bfloat16)
    top_pre = jnp.dot(second_act, weight_out, preferred_element_type=jnp.float32)
    centred = top_pre - lax.optimization_barrier(jnp.mean(top_pre, axis=-1, keepdims=True))
    inverse = lax.rsqrt(lax.optimization_barrier(jnp.mean(centred * centred, axis=-1, keepdims=True)) + epsilon)
    normed = centred * inverse
    return (normed, (first_pre, first_act, second_pre, second_act, normed, inverse))

def mlp_backward(inputs, stored, upstream, weight_in, weight_mid, weight_out):
    first_pre, first_act, second_pre, second_act, normed, inverse = stored
    top_grad = inverse * (upstream - lax.optimization_barrier(jnp.mean(upstream, axis=-1, keepdims=True)) - normed * lax.optimization_barrier(jnp.mean(upstream * normed, axis=-1, keepdims=True)))
    top_grad = top_grad.astype(jnp.bfloat16)
    out_wgrad = jnp.dot(second_act.T, top_grad, preferred_element_type=jnp.float32)
    second_grad = jnp.dot(top_grad, weight_out.T, preferred_element_type=jnp.float32)
    second_grad = (second_grad * silu_slope(second_pre)).astype(jnp.bfloat16)
    mid_wgrad = jnp.dot(first_act.T, second_grad, preferred_element_type=jnp.float32)
    first_grad = jnp.dot(second_grad, weight_mid.T, preferred_element_type=jnp.float32)
    first_grad = (first_grad * silu_slope(first_pre)).astype(jnp.bfloat16)
    in_wgrad = jnp.dot(inputs.T, first_grad, preferred_element_type=jnp.float32)
    input_grad = jnp.dot(first_grad, weight_in.T, preferred_element_type=jnp.float32)
    return (input_grad, (in_wgrad, mid_wgrad, out_wgrad))

def partition_backward(weights, call_arguments):
    own_latent, border_state, edge_rows, node_cot, edge_cot, sender_ids, receiver_ids, live_count = call_arguments
    features = own_latent.shape[1]
    node_rows = own_latent.shape[0]
    extended = jnp.concatenate([own_latent, border_state], 0)
    edge_inputs = jnp.concatenate([edge_rows, extended[sender_ids], own_latent[receiver_ids]], 1)
    edge_out, edge_stored = mlp_forward(edge_inputs, weights[0], weights[1], weights[2])
    live_mask = (jnp.arange(edge_rows.shape[0], dtype=jnp.int32) < live_count)[:, None]
    message = jnp.where(live_mask, edge_out, 0.0).astype(jnp.bfloat16)
    message = lax.optimization_barrier(message).astype(jnp.float32)
    aggregate = jax.ops.segment_sum(message, receiver_ids, num_segments=node_rows).astype(jnp.bfloat16)
    node_inputs = jnp.concatenate([own_latent, aggregate], 1)
    node_stored = mlp_forward(node_inputs, weights[3], weights[4], weights[5])[1]
    node_input_grad, node_wgrads = mlp_backward(node_inputs, node_stored, node_cot.astype(jnp.float32), weights[3], weights[4], weights[5])
    aggregate_grad = node_input_grad[:, features:]
    cotangent = edge_cot.astype(jnp.float32)
    edge_upstream = jnp.where(live_mask, cotangent + aggregate_grad[receiver_ids], 0.0)
    edge_input_grad, edge_wgrads = mlp_backward(edge_inputs, edge_stored, edge_upstream, weights[0], weights[1], weights[2])
    edge_grad = jnp.where(live_mask, cotangent + edge_input_grad[:, :features], 0.0).astype(jnp.bfloat16)
    widened_gradient = jnp.zeros((extended.shape[0], features), jnp.float32)
    widened_gradient = widened_gradient.at[sender_ids].add(edge_input_grad[:, features:2 * features])
    widened_gradient = widened_gradient.at[receiver_ids].add(edge_input_grad[:, 2 * features:])
    widened_gradient = widened_gradient.at[:node_rows].add(node_cot.astype(jnp.float32) + node_input_grad[:, :features])
    return (widened_gradient, edge_grad, edge_wgrads + node_wgrads)

def pick_rows(table, indices):
    return table[indices]

def scatter_rows(table, indices, values):
    return table.at[indices].add(values)

def shift_down(values, axis):
    length = values.shape[axis]
    filler = jnp.zeros_like(lax.slice_in_dim(values, 0, 1, axis=axis))
    return jnp.concatenate([filler, lax.slice_in_dim(values, 0, length - 1, axis=axis)], axis)

def shift_up(values, axis):
    length = values.shape[axis]
    filler = jnp.zeros_like(lax.slice_in_dim(values, 0, 1, axis=axis))
    return jnp.concatenate([lax.slice_in_dim(values, 1, length, axis=axis), filler], axis)

def adjacent_blocks(blocks):
    return jnp.stack([shift_down(blocks[:, :, 1], 0), shift_up(blocks[:, :, 0], 0), shift_down(blocks[:, :, 3], 1), shift_up(blocks[:, :, 2], 1)], axis=2)

def reference(node_hidden_state, edge_hidden_state, node_output_gradient, edge_output_gradient, senders, receivers, edge_slot_count, outbound_rows, edge_weight_in, edge_weight_mid, edge_weight_out, node_weight_in, node_weight_mid, node_weight_out):
    grid_latent = node_hidden_state.reshape(N_WIDE, N_NARROW, PART_NODE_COUNT, LATENT_WIDTH)
    grid_lists = outbound_rows.reshape(N_WIDE, N_NARROW, 4, BORDER_NODES)
    shipped_rows = jax.vmap(jax.vmap(pick_rows))(grid_latent, grid_lists)
    border_state = adjacent_blocks(shipped_rows).reshape(GRAPH_PIECES, 4 * BORDER_NODES, LATENT_WIDTH)
    weights = (edge_weight_in, edge_weight_mid, edge_weight_out, node_weight_in, node_weight_mid, node_weight_out)
    call_arguments = (node_hidden_state.reshape(GRAPH_PIECES, PART_NODE_COUNT, LATENT_WIDTH), border_state, edge_hidden_state.reshape(GRAPH_PIECES, PART_EDGE_SLOTS, LATENT_WIDTH), node_output_gradient.reshape(GRAPH_PIECES, PART_NODE_COUNT, LATENT_WIDTH), edge_output_gradient.reshape(GRAPH_PIECES, PART_EDGE_SLOTS, LATENT_WIDTH), senders.reshape(GRAPH_PIECES, PART_EDGE_SLOTS), receivers.reshape(GRAPH_PIECES, PART_EDGE_SLOTS), edge_slot_count)
    widened_gradient, edge_grad, wgrads = lax.map(partial(partition_backward, weights), call_arguments)
    border_gradient = widened_gradient[:, PART_NODE_COUNT:].reshape(N_WIDE, N_NARROW, 4, BORDER_NODES, LATENT_WIDTH)
    results_back = adjacent_blocks(border_gradient).reshape(GRAPH_PIECES, 4 * BORDER_NODES, LATENT_WIDTH)
    node_state_gradient = jax.vmap(scatter_rows)(widened_gradient[:, :PART_NODE_COUNT], outbound_rows.reshape(GRAPH_PIECES, 4 * BORDER_NODES), results_back)
    edge_scale = 1.0 / math.sqrt(EDGES)
    node_scale = 1.0 / math.sqrt(NODES)
    summed = [lax.optimization_barrier(jnp.sum(values, axis=0)) for values in wgrads]
    return (node_state_gradient.reshape(NODES, LATENT_WIDTH), edge_grad.reshape(EDGES, LATENT_WIDTH), summed[0] * edge_scale, summed[1] * edge_scale, summed[2] * edge_scale, summed[3] * node_scale, summed[4] * node_scale, summed[5] * node_scale)
```

```python
import functools
import math

import jax
import jax.numpy as jnp
from jax import lax
from jax.experimental import pallas as pl
from jax.experimental.pallas import tpu as pltpu
from jax.sharding import PartitionSpec as P

F32 = jnp.float32
BF16 = jnp.bfloat16
MESH = pl.DeviceIdType.MESH
EPS = 1e-05

D = 128
NODES = 2048
HALO = 512
EDGES = 12288
BLOCK = 1024
CHUNK = 256
BLOCKS = EDGES // BLOCK
CHUNKS = BLOCK // CHUNK
WINDOW = 256
LANES = 128
ROWS = BLOCK // LANES
PADDED = NODES + WINDOW
W_ROWS = 1280
VMEM_LIMIT = 62 * 1024 * 1024


def mm(a, b):
    return jnp.dot(a, b, preferred_element_type=F32)


def mm_t(a, b):
    return lax.dot_general(a, b, (((1,), (1,)), ((), ())), preferred_element_type=F32)


def t_mm(a, b):
    return lax.dot_general(a, b, (((0,), (0,)), ((), ())), preferred_element_type=F32)


def silu_pair(v):
    s = 0.5 * jnp.tanh(0.5 * v) + 0.5
    a = v * s
    return a.astype(BF16), (s + a * (1.0 - s)).astype(BF16)


def normalise(top):
    centred = top - jnp.mean(top, axis=-1, keepdims=True)
    inverse = lax.rsqrt(jnp.mean(centred * centred, axis=-1, keepdims=True) + EPS)
    return centred * inverse, inverse


def norm_grad(g, normed, inverse):
    return inverse * (
        g
        - jnp.mean(g, axis=-1, keepdims=True)
        - normed * jnp.mean(g * normed, axis=-1, keepdims=True)
    )


def columns_of(row):
    return jnp.transpose(jnp.broadcast_to(row, (LANES, LANES)))


def hot(mask):
    return jnp.where(mask, jnp.ones((), BF16), jnp.zeros((), BF16))


def partition_kernel(
    count_ref, recv_sm, node_ref, halo_ref, ncot_ref, edge_hbm, cot_hbm, send_ref, recv_ref,
    ewi_ref, ewm_ref, ewo_ref, nwi_ref, nwm_ref, nwo_ref,
    egrad_hbm, own_ref, border_ref, wg_ref,
    edge_v, cot_v, egrad_v, s2, rtab, agg, agtab, f2, frecv, a1, d1, a2, d2, nrm, inv, hotr, side,
    tgs, sgs, fgs, fg2, iota_r, iota_c, wge, wgm, wgo, wni, wnm, wno, sem_e, sem_c, sem_g,
):
    count = count_ref[0]

    def block_copy(hbm, v, sem, b):
        at = pl.ds(b * BLOCK, BLOCK)
        return pltpu.make_async_copy(hbm.at[at, :], v.at[at, :], sem.at[b])

    def out_copy(b):
        at = pl.ds(b * BLOCK, BLOCK)
        return pltpu.make_async_copy(egrad_v.at[at, :], egrad_hbm.at[at, :], sem_g.at[b])

    @pl.loop(0, BLOCKS)
    def _(b):
        block_copy(edge_hbm, edge_v, sem_e, b).start()

    @pl.loop(0, BLOCKS)
    def _(b):
        block_copy(cot_hbm, cot_v, sem_c, b).start()

    own_rows = pl.ds(0, NODES)
    w_e, w_s, w_r = ewi_ref[0:D], ewi_ref[D : 2 * D], ewi_ref[2 * D : 3 * D]

    @pl.loop(0, NODES // CHUNK)
    def _(i):
        at = pl.ds(i * CHUNK, CHUNK)
        s2[at, 0:D] = mm(node_ref[at, :], w_s).astype(BF16)
        s2[at, D : 2 * D] = mm(halo_ref[at, :], w_s).astype(BF16)
        rtab[at, :] = mm(node_ref[at, :], w_r).astype(BF16)
        iota_c[at, :] = (
            lax.broadcasted_iota(jnp.int32, (CHUNK, LANES), 0) + i * CHUNK
        ).astype(jnp.int16)

    iota_r[...] = lax.broadcasted_iota(jnp.int32, (16, NODES), 1).astype(jnp.int16)
    rtab[pl.ds(NODES, WINDOW), :] = jnp.zeros((WINDOW, D), BF16)
    agtab[pl.ds(NODES, WINDOW), :] = jnp.zeros((WINDOW, D), BF16)
    agg[...] = jnp.zeros_like(agg)
    frecv[...] = jnp.zeros_like(frecv)
    f2[...] = jnp.zeros_like(f2)
    for ref in (wge, wgm, wgo, wni, wnm, wno):
        ref[...] = jnp.zeros_like(ref)

    def window_of(b):
        start = pl.multiple_of((recv_sm[b * ROWS, 0] // 16) * 16, 16)
        windows = (recv_sm[b * ROWS + ROWS - 1, LANES - 1] - start) // WINDOW + 1
        return start, windows

    def tile_hot(col16, width):
        tiles = []
        for r in range(LANES // 16):
            part = col16[r * 16 : r * 16 + 16]
            tiles.append(
                jnp.concatenate(
                    [
                        hot(part == iota_r[:, t * LANES : (t + 1) * LANES])
                        for t in range(width // LANES)
                    ],
                    axis=1,
                )
            )
        return jnp.concatenate(tiles, axis=0)

    def row_hot(row, height):
        row16 = jnp.broadcast_to(row, (16, LANES)).astype(jnp.int16)
        return jnp.concatenate(
            [hot(row16 == iota_c[k * 16 : k * 16 + 16, :]) for k in range(height // 16)], axis=0
        )

    def receiver_hot(b, start, extra):
        parts = []
        for r in range(ROWS):
            row = recv_ref[pl.ds(b * ROWS + r, 1), :] - start
            place = b * BLOCK + r * LANES + lax.broadcasted_iota(jnp.int32, (1, LANES), 1)
            row = jnp.where((place < count) & (row >= 0) & (row < WINDOW), row, -1)
            parts.append(row_hot(row, WINDOW))
        return jnp.concatenate(parts, axis=1)

    def column_hot_windows(col, start, k):
        local = col - (start + k * WINDOW)
        local = jnp.where((local >= 0) & (local < WINDOW), local, -1).astype(jnp.int16)
        return tile_hot(local, WINDOW)

    def forward_block(b, single):
        start, windows = window_of(b)
        for c in range(CHUNKS):
            at = pl.ds(b * BLOCK + c * CHUNK, CHUNK)
            send_hots, recv_cols, sides = [], [], []
            for r in range(CHUNK // LANES):
                line = pl.ds(b * ROWS + c * (CHUNK // LANES) + r, 1)
                packed = columns_of(send_ref[line, :] + (recv_ref[line, :] << 12))
                sender = packed & 4095
                recv_cols.append(packed >> 12)
                sides.append(sender >= NODES)
                send_hots.append(tile_hot((sender & (NODES - 1)).astype(jnp.int16), NODES))
            picked = mm(jnp.concatenate(send_hots, axis=0), s2[...])
            far = jnp.concatenate(sides, axis=0)
            pre = jnp.where(far, picked[:, D:], picked[:, :D]) + mm(edge_v[at, :], w_e)
            side[at, :] = jnp.where(far, 1.0, 0.0).astype(BF16)
            if single:
                near = jnp.concatenate([column_hot_windows(x, start, 0) for x in recv_cols], axis=0)
                hotr[at, :] = near
                pre = pre + mm(near, rtab[pl.ds(start, WINDOW), :])
            else:

                def add(k, total):
                    near = jnp.concatenate(
                        [column_hot_windows(x, start, k) for x in recv_cols], axis=0
                    )
                    place = pl.multiple_of(start + k * WINDOW, 16)
                    return total + mm(near, rtab[pl.ds(place, WINDOW), :])

                pre = lax.fori_loop(0, windows, add, pre)
            act1, slope1 = silu_pair(pre)
            a1[at, :] = act1
            d1[at, :] = slope1
            act2, slope2 = silu_pair(mm(act1, ewm_ref[...]))
            a2[at, :] = act2
            d2[at, :] = slope2
            normed, inverse = normalise(mm(act2, ewo_ref[...]))
            nrm[at, :] = normed.astype(BF16)
            inv[at, :] = jnp.broadcast_to(inverse, (CHUNK, D))
        rows = pl.ds(b * BLOCK, BLOCK)

        def send_on(k, carry):
            place = pl.multiple_of(start + k * WINDOW, 16)
            into = pl.ds(place, WINDOW)
            agg[into, :] += mm(receiver_hot(b, place, None), nrm[rows, :])
            return carry

        if single:
            send_on(0, 0)
        else:
            lax.fori_loop(0, windows, send_on, 0)

    @pl.loop(0, BLOCKS)
    def _(b):
        block_copy(edge_hbm, edge_v, sem_e, b).wait()
        windows = window_of(b)[1]
        live = b * BLOCK < count

        @pl.when(live & (windows == 1))
        def _():
            forward_block(b, True)

        @pl.when(live & (windows > 1))
        def _():
            forward_block(b, False)

    @pl.loop(0, NODES // CHUNK)
    def _(i):
        at = pl.ds(i * CHUNK, CHUNK)
        own = node_ref[at, :]
        total = agg[at, :].astype(BF16)
        inputs = jnp.concatenate([own, total], axis=1)
        act1, slope1 = silu_pair(mm(inputs, nwi_ref[...]))
        act2, slope2 = silu_pair(mm(act1, nwm_ref[...]))
        normed, inverse = normalise(mm(act2, nwo_ref[...]))
        g = ncot_ref[at, :].astype(F32)
        top = norm_grad(g, normed, inverse).astype(BF16)
        wno[...] += t_mm(act2, top)
        second = (mm_t(top, nwo_ref[...]) * slope2.astype(F32)).astype(BF16)
        wnm[...] += t_mm(act1, second)
        first = (mm_t(second, nwm_ref[...]) * slope1.astype(F32)).astype(BF16)
        wni[...] += t_mm(inputs, first)
        back = mm_t(first, nwi_ref[...])
        own_ref[at, :] = g + back[:, :D]
        agtab[at, :] = back[:, D:].astype(BF16)

    def backward_block(b, single):
        start, windows = window_of(b)
        for c in range(CHUNKS):
            at = pl.ds(b * BLOCK + c * CHUNK, CHUNK)
            here = pl.ds(c * CHUNK, CHUNK)
            cot = cot_v[at, :].astype(F32)
            if single:
                g = cot + mm(hotr[at, :], agtab[pl.ds(start, WINDOW), :])
            else:
                cols = []
                for r in range(CHUNK // LANES):
                    line = pl.ds(b * ROWS + c * (CHUNK // LANES) + r, 1)
                    cols.append(columns_of(recv_ref[line, :]))

                def add(k, total):
                    near = jnp.concatenate([column_hot_windows(x, start, k) for x in cols], axis=0)
                    place = pl.multiple_of(start + k * WINDOW, 16)
                    return total + mm(near, agtab[pl.ds(place, WINDOW), :])

                g = lax.fori_loop(0, windows, add, cot)
            place = b * BLOCK + c * CHUNK + lax.broadcasted_iota(jnp.int32, (CHUNK, D), 0)
            live = place < count
            top = norm_grad(g, nrm[at, :].astype(F32), inv[at, :])
            top = jnp.where(live, top, 0.0).astype(BF16)
            tgs[here, :] = top
            second = (mm_t(top, ewo_ref[...]) * d2[at, :].astype(F32)).astype(BF16)
            sgs[here, :] = second
            first = (mm_t(second, ewm_ref[...]) * d1[at, :].astype(F32)).astype(BF16)
            fgs[here, :] = first
            far = first * side[at, :]
            fg2[here, D : 2 * D] = far
            fg2[here, 0:D] = first - far
            grad = cot + mm_t(first, w_e)
            egrad_v[at, :] = jnp.where(live, grad, 0.0).astype(BF16)
        out_copy(b).start()
        rows = pl.ds(b * BLOCK, BLOCK)
        wgo[...] += t_mm(a2[rows, :], tgs[...])
        wgm[...] += t_mm(a1[rows, :], sgs[...])
        wge[...] += t_mm(edge_v[rows, :], fgs[...])

        def send_on(k, carry):
            place = pl.multiple_of(start + k * WINDOW, 16)
            into = pl.ds(place, WINDOW)
            frecv[into, :] += mm(receiver_hot(b, place, None), fgs[...])
            return carry

        if single:
            send_on(0, 0)
        else:
            lax.fori_loop(0, windows, send_on, 0)
        f2[...] += mm(
            jnp.concatenate(
                [
                    row_hot(send_ref[pl.ds(b * ROWS + r, 1), :] & (NODES - 1), NODES)
                    for r in range(ROWS)
                ],
                axis=1,
            ),
            fg2[...],
        )

    @pl.loop(0, BLOCKS)
    def _(b):
        block_copy(cot_hbm, cot_v, sem_c, b).wait()
        windows = window_of(b)[1]
        live = b * BLOCK < count

        @pl.when(live & (windows == 1))
        def _():
            backward_block(b, True)

        @pl.when(live & (windows > 1))
        def _():
            backward_block(b, False)

        @pl.when(jnp.logical_not(live))
        def _():
            egrad_v[pl.ds(b * BLOCK, BLOCK), :] = jnp.zeros((BLOCK, D), BF16)
            out_copy(b).start()

    wg_ref[D : 2 * D, :] = jnp.zeros((D, D), BF16)
    wsend = jnp.zeros((D, D), F32)
    wrecv = jnp.zeros((D, D), F32)
    for i in range(NODES // BLOCK):
        at = pl.ds(i * BLOCK, BLOCK)
        near = f2[at, 0:D].astype(BF16)
        far = f2[at, D : 2 * D].astype(BF16)
        recv = frecv[at, :].astype(BF16)
        own_ref[at, :] += mm_t(near, w_s) + mm_t(recv, w_r)
        border_ref[at, :] = mm_t(far, w_s).astype(BF16)
        wsend = wsend + t_mm(node_ref[at, :], near) + t_mm(halo_ref[at, :], far)
        wrecv = wrecv + t_mm(node_ref[at, :], recv)
    wg_ref[0:D, :] = wge[...].astype(BF16)
    wg_ref[D : 2 * D, :] = wsend.astype(BF16)
    wg_ref[2 * D : 3 * D, :] = wrecv.astype(BF16)
    wg_ref[3 * D : 4 * D, :] = wgm[...].astype(BF16)
    wg_ref[4 * D : 5 * D, :] = wgo[...].astype(BF16)
    wg_ref[5 * D : 7 * D, :] = wni[...].astype(BF16)
    wg_ref[7 * D : 8 * D, :] = wnm[...].astype(BF16)
    wg_ref[8 * D : 9 * D, :] = wno[...].astype(BF16)
    wg_ref[9 * D : 10 * D, :] = jnp.zeros((D, D), BF16)

    @pl.loop(0, BLOCKS)
    def _(b):
        out_copy(b).wait()


def partition_call(count, node, halo, ncot, edge, cot, send, recv, weights):
    vm = pl.BlockSpec(memory_space=pltpu.VMEM)
    sm = pl.BlockSpec(memory_space=pltpu.SMEM)
    hb = pl.BlockSpec(memory_space=pl.ANY)
    v = pltpu.VMEM
    return pl.pallas_call(
        partition_kernel,
        out_shape=(
            jax.ShapeDtypeStruct((EDGES, D), BF16),
            jax.ShapeDtypeStruct((NODES, D), F32),
            jax.ShapeDtypeStruct((NODES, D), BF16),
            jax.ShapeDtypeStruct((W_ROWS, D), BF16),
        ),
        in_specs=[sm, sm, vm, vm, vm, hb, hb, vm, vm] + [vm] * 6,
        out_specs=(hb, vm, vm, vm),
        scratch_shapes=[
            v((EDGES, D), BF16), v((EDGES, D), BF16), v((EDGES, D), BF16),
            v((NODES, 2 * D), BF16), v((PADDED, D), BF16), v((PADDED, D), F32), v((PADDED, D), BF16),
            v((NODES, 2 * D), F32), v((PADDED, D), F32),
            v((EDGES, D), BF16), v((EDGES, D), BF16), v((EDGES, D), BF16), v((EDGES, D), BF16),
            v((EDGES, D), BF16), v((EDGES, D), F32), v((EDGES, WINDOW), BF16), v((EDGES, D), BF16),
            v((BLOCK, D), BF16), v((BLOCK, D), BF16), v((BLOCK, D), BF16), v((BLOCK, 2 * D), BF16),
            v((16, NODES), jnp.int16), v((NODES, LANES), jnp.int16),
            v((D, D), F32), v((D, D), F32), v((D, D), F32),
            v((2 * D, D), F32), v((D, D), F32), v((D, D), F32),
            pltpu.SemaphoreType.DMA((BLOCKS,)), pltpu.SemaphoreType.DMA((BLOCKS,)),
            pltpu.SemaphoreType.DMA((BLOCKS,)),
        ],
        compiler_params=pltpu.CompilerParams(vmem_limit_bytes=VMEM_LIMIT),
        name="partition",
    )(count, recv, node, halo, ncot, edge, cot, send, recv, *weights)


def cell(w, v):
    return {"wide": w, "narrow": v}


def swap_halos(w, v, wide, narrow, blocks, landing, send_sem, recv_sem):
    sides = (
        (w > 0, cell(w - 1, v)),
        (w < wide - 1, cell(w + 1, v)),
        (v > 0, cell(w, v - 1)),
        (v < narrow - 1, cell(w, v + 1)),
    )

    def copy(j):
        return pltpu.make_async_remote_copy(
            src_ref=blocks(j),
            dst_ref=landing.at[pl.ds((j ^ 1) * HALO, HALO), :],
            send_sem=send_sem.at[j],
            recv_sem=recv_sem.at[j ^ 1],
            device_id=sides[j][1],
            device_id_type=MESH,
        )

    def arrival(j):
        return pltpu.make_async_remote_copy(
            src_ref=blocks(j),
            dst_ref=landing.at[pl.ds(j * HALO, HALO), :],
            send_sem=send_sem.at[j],
            recv_sem=recv_sem.at[j],
            device_id=sides[j][1],
            device_id_type=MESH,
        )

    return sides, copy, arrival


def halo_kernel(wide, narrow, node_ref, out_rows_ref, halo_ref, outgoing, landing, send_sem, recv_sem):
    w, v = lax.axis_index("wide"), lax.axis_index("narrow")
    sides, copy, arrival = swap_halos(
        w, v, wide, narrow, lambda j: outgoing.at[pl.ds(j * HALO, HALO), :], landing, send_sem, recv_sem
    )
    barrier = pltpu.get_barrier_semaphore()
    for j in range(4):

        @pl.when(sides[j][0])
        def _():
            pl.semaphore_signal(barrier, inc=1, device_id=sides[j][1], device_id_type=MESH)

    iota = lax.broadcasted_iota(jnp.int32, (LANES, NODES), 1).astype(jnp.int16)

    def gather(j):
        hots = []
        for c in range(HALO // LANES):
            col = columns_of(out_rows_ref[j : j + 1, c * LANES : (c + 1) * LANES]).astype(jnp.int16)
            hots.append(
                jnp.concatenate(
                    [hot(col == iota[:, t * LANES : (t + 1) * LANES]) for t in range(NODES // LANES)],
                    axis=1,
                )
            )
        outgoing[pl.ds(j * HALO, HALO), :] = mm(jnp.concatenate(hots, axis=0), node_ref[...]).astype(BF16)

    for j in range(4):
        gather(j)
        if j == 0:
            peers = sum(s[0].astype(jnp.int32) for s in sides)
            pl.semaphore_wait(barrier, peers)

        @pl.when(sides[j][0])
        def _():
            copy(j).start()

    for j in range(4):
        rows = pl.ds(j * HALO, HALO)

        @pl.when(sides[j][0])
        def _():
            copy(j).wait_send()
            arrival(j).wait_recv()
            halo_ref[rows, :] = landing[rows, :]

        @pl.when(jnp.logical_not(sides[j][0]))
        def _():
            halo_ref[rows, :] = jnp.zeros((HALO, D), BF16)


def halo_call(wide, narrow, node, out_rows):
    vm = pl.BlockSpec(memory_space=pltpu.VMEM)
    return pl.pallas_call(
        functools.partial(halo_kernel, wide, narrow),
        out_shape=jax.ShapeDtypeStruct((4 * HALO, D), BF16),
        in_specs=[vm, vm],
        out_specs=vm,
        scratch_shapes=[
            pltpu.VMEM((4 * HALO, D), BF16),
            pltpu.VMEM((4 * HALO, D), BF16),
            pltpu.SemaphoreType.DMA((4,)),
            pltpu.SemaphoreType.DMA((4,)),
        ],
        compiler_params=pltpu.CompilerParams(
            collective_id=0, has_side_effects=True, vmem_limit_bytes=VMEM_LIMIT
        ),
        name="halo",
    )(node, out_rows)


def reduce_kernel(
    wide, narrow, border_ref, wg_ref, back_ref, sum_ref,
    landing, first, second, part, third, send_h, recv_h, send_1, recv_1, send_2, recv_2, send_3, recv_3,
):
    w, v = lax.axis_index("wide"), lax.axis_index("narrow")
    piece = W_ROWS // wide
    sides, copy, arrival = swap_halos(
        w, v, wide, narrow, lambda j: border_ref.at[pl.ds(j * HALO, HALO), :], landing, send_h, recv_h
    )
    barrier = pltpu.get_barrier_semaphore()
    for p in range(1, wide):
        pl.semaphore_signal(barrier, inc=1, device_id=cell(lax.rem(w + p, wide), v), device_id_type=MESH)
    for p in range(1, narrow):
        pl.semaphore_signal(barrier, inc=1, device_id=cell(w, lax.rem(v + p, narrow)), device_id_type=MESH)
    pl.semaphore_wait(barrier, wide + narrow - 2)

    def rows_of(i):
        return pl.ds(pl.multiple_of(i * piece, 16), piece)

    def send(src, dst, send_sem, recv_sem, device):
        return pltpu.make_async_remote_copy(
            src_ref=src, dst_ref=dst, send_sem=send_sem, recv_sem=recv_sem, device_id=device,
            device_id_type=MESH,
        )

    scatter, share, spread = [], [], []
    for p in range(1, wide):
        to = lax.rem(w + p, wide)
        scatter.append(
            send(wg_ref.at[rows_of(to), :], first.at[p], send_1.at[p], recv_1.at[p], cell(to, v))
        )
        scatter[-1].start()
    for j in range(4):

        @pl.when(sides[j][0])
        def _():
            copy(j).start()

    total = wg_ref[rows_of(w), :].astype(F32)
    for p in range(1, wide):
        scatter[p - 1].wait_recv()
        total = total + first[p].astype(F32)
    part[...] = total.astype(BF16)
    for p in range(1, narrow):
        to = lax.rem(v + p, narrow)
        share.append(send(part, second.at[v], send_2.at[p], recv_2.at[p], cell(w, to)))
        share[-1].start()
    second[v] = part[...]
    for p in range(1, narrow):
        share[p - 1].wait_recv()
    total = second[0].astype(F32)
    for i in range(1, narrow):
        total = total + second[i].astype(F32)
    third[rows_of(w), :] = total.astype(BF16)
    for p in range(1, wide):
        to = lax.rem(w + p, wide)
        spread.append(
            send(
                third.at[rows_of(w), :], third.at[rows_of(w), :], send_3.at[p], recv_3.at[p], cell(to, v)
            )
        )
        spread[-1].start()
    for j in range(4):
        rows = pl.ds(j * HALO, HALO)

        @pl.when(sides[j][0])
        def _():
            copy(j).wait_send()
            arrival(j).wait_recv()
            back_ref[rows, :] = landing[rows, :]

        @pl.when(jnp.logical_not(sides[j][0]))
        def _():
            back_ref[rows, :] = jnp.zeros((HALO, D), BF16)

    for p in range(1, wide):
        spread[p - 1].wait_recv()
    sum_ref[...] = third[...]
    for c in scatter + share + spread:
        c.wait_send()


def reduce_call(wide, narrow, border, wg):
    vm = pl.BlockSpec(memory_space=pltpu.VMEM)
    piece = W_ROWS // wide
    sem = pltpu.SemaphoreType.DMA
    return pl.pallas_call(
        functools.partial(reduce_kernel, wide, narrow),
        out_shape=(
            jax.ShapeDtypeStruct((4 * HALO, D), BF16),
            jax.ShapeDtypeStruct((W_ROWS, D), BF16),
        ),
        in_specs=[vm, vm],
        out_specs=(vm, vm),
        scratch_shapes=[
            pltpu.VMEM((4 * HALO, D), BF16),
            pltpu.VMEM((wide, piece, D), BF16),
            pltpu.VMEM((narrow, piece, D), BF16),
            pltpu.VMEM((piece, D), BF16),
            pltpu.VMEM((W_ROWS, D), BF16),
            sem((4,)), sem((4,)), sem((wide,)), sem((wide,)), sem((narrow,)), sem((narrow,)),
            sem((wide,)), sem((wide,)),
        ],
        compiler_params=pltpu.CompilerParams(
            collective_id=1, has_side_effects=True, vmem_limit_bytes=VMEM_LIMIT
        ),
        name="reduce",
    )(border, wg)


def finish_kernel(scales, out_rows_ref, own_ref, back_ref, sum_ref, node_ref, *outs):
    for i in range(NODES // CHUNK):
        at = pl.ds(i * CHUNK, CHUNK)
        iota = (lax.broadcasted_iota(jnp.int32, (CHUNK, LANES), 0) + i * CHUNK).astype(jnp.int16)
        hots = []
        for j in range(4):
            for c in range(HALO // LANES):
                row = out_rows_ref[j : j + 1, c * LANES : (c + 1) * LANES]
                row16 = jnp.broadcast_to(row, (CHUNK, LANES)).astype(jnp.int16)
                hots.append(hot(row16 == iota))
        node_ref[at, :] = own_ref[at, :] + mm(jnp.concatenate(hots, axis=1), back_ref[...])
    at = 0
    for out, scale in zip(outs, scales):
        rows = out.shape[0]
        out[...] = sum_ref[at : at + rows, :].astype(F32) * scale
        at += rows


def finish_call(scales, out_rows, own, back, summed, shapes):
    vm = pl.BlockSpec(memory_space=pltpu.VMEM)
    return pl.pallas_call(
        functools.partial(finish_kernel, scales),
        out_shape=(jax.ShapeDtypeStruct((NODES, D), F32),)
        + tuple(jax.ShapeDtypeStruct(s, F32) for s in shapes),
        in_specs=[vm] * 4,
        out_specs=(vm,) * 7,
        compiler_params=pltpu.CompilerParams(vmem_limit_bytes=VMEM_LIMIT),
        name="finish",
    )(out_rows, own, back, summed)


def per_device(
    wide,
    narrow,
    node_hidden_state,
    edge_hidden_state,
    node_output_gradient,
    edge_output_gradient,
    senders,
    receivers,
    edge_slot_count,
    outbound_rows,
    *weights,
):
    out_rows = outbound_rows.reshape(4, HALO)
    halo = halo_call(wide, narrow, node_hidden_state, out_rows)
    edge_grad, own, border, wg = partition_call(
        edge_slot_count,
        node_hidden_state,
        halo,
        node_output_gradient,
        edge_hidden_state,
        edge_output_gradient,
        senders.reshape(EDGES // LANES, LANES),
        receivers.reshape(EDGES // LANES, LANES),
        weights,
    )
    back, summed = reduce_call(wide, narrow, border, wg)
    edge_scale = 1.0 / math.sqrt(EDGES * wide * narrow)
    node_scale = 1.0 / math.sqrt(NODES * wide * narrow)
    node_grad, *sums = finish_call(
        (edge_scale,) * 3 + (node_scale,) * 3, out_rows, own, back, summed, [x.shape for x in weights]
    )
    return (node_grad, edge_grad, *sums)


def solution(mesh):
    both = ("wide", "narrow")
    rows, flat = P(both, None), P(both)
    return jax.shard_map(
        functools.partial(per_device, mesh.shape["wide"], mesh.shape["narrow"]),
        mesh=mesh,
        in_specs=(rows, rows, rows, rows, flat, flat, flat, P(both, None, None)) + (P(),) * 6,
        out_specs=(rows, rows) + (P(),) * 6,
        check_vma=False,
    )
```

```python
import functools
import math

import jax
import jax.numpy as jnp
from jax import lax
from jax.experimental import pallas as pl
from jax.experimental.pallas import tpu as pltpu
from jax.sharding import PartitionSpec as P

F32 = jnp.float32
BF16 = jnp.bfloat16
MESH = pl.DeviceIdType.MESH
EPS = 1e-05

D = 128
NODES = 2048
HALO = 512
EDGES = 12288
BLOCK = 1024
CHUNK = 1024
NODE_CHUNK = 1024
BLOCKS = EDGES // BLOCK
CHUNKS = BLOCK // CHUNK
WINDOW = 256
LANES = 128
ROWS = BLOCK // LANES
PADDED = NODES + WINDOW
W_ROWS = 1280
EARLY = 4
VMEM_LIMIT = 62 * 1024 * 1024


def mm(a, b):
    return jnp.dot(a, b, preferred_element_type=F32)


def mm_t(a, b):
    return lax.dot_general(a, b, (((1,), (1,)), ((), ())), preferred_element_type=F32)


def t_mm(a, b):
    return lax.dot_general(a, b, (((0,), (0,)), ((), ())), preferred_element_type=F32)


def silu_pair(v):
    s = 0.5 * jnp.tanh(0.5 * v) + 0.5
    a = v * s
    return a.astype(BF16), (s + a * (1.0 - s)).astype(BF16)


def normalise(top):
    centred = top - jnp.mean(top, axis=-1, keepdims=True)
    inverse = lax.rsqrt(jnp.mean(centred * centred, axis=-1, keepdims=True) + EPS)
    return centred * inverse, inverse


def norm_grad(g, normed, inverse):
    return inverse * (
        g
        - jnp.mean(g, axis=-1, keepdims=True)
        - normed * jnp.mean(g * normed, axis=-1, keepdims=True)
    )


def columns_of(row):
    return jnp.transpose(jnp.broadcast_to(row, (LANES, LANES)))


def hot(mask):
    return jnp.where(mask, jnp.ones((), BF16), jnp.zeros((), BF16))


def partition_kernel(
    count_ref, recv_sm, node_ref, ncot_ref, edge_hbm, cot_hbm, picked_hbm, recv_ref,
    ewi_ref, ewm_ref, ewo_ref, nwi_ref, nwm_ref, nwo_ref,
    egrad_hbm, first_hbm, own_ref, wg_ref,
    edge_v, cot_v, picked_v, first_v, rtab, agg, agtab, frecv, a1, d1, a2, d2, nrm, inv, hotr,
    tgs, sgs, iota_r, iota_c, wge, wgm, wgo, wni, wnm, wno, sem_e, sem_c, sem_p, sem_g, sem_f,
):
    count = count_ref[0]

    def block_copy(hbm, v, sem, b):
        at = pl.ds(b * BLOCK, BLOCK)
        return pltpu.make_async_copy(hbm.at[at, :], v.at[at, :], sem.at[b])

    def out_copy(b):
        at = pl.ds(b * BLOCK, BLOCK)
        return pltpu.make_async_copy(cot_v.at[at, :], egrad_hbm.at[at, :], sem_g.at[b])

    def first_copy(b):
        at = pl.ds(b * BLOCK, BLOCK)
        return pltpu.make_async_copy(first_v.at[at, :], first_hbm.at[at, :], sem_f.at[b])

    @pl.loop(0, BLOCKS)
    def _(b):
        block_copy(edge_hbm, edge_v, sem_e, b).start()
        block_copy(picked_hbm, picked_v, sem_p, b).start()

    @pl.loop(0, BLOCKS)
    def _(b):
        block_copy(cot_hbm, cot_v, sem_c, b).start()

    w_e, w_es, w_r = ewi_ref[0:D], ewi_ref[0 : 2 * D], ewi_ref[2 * D : 3 * D]

    for i in range(NODES // NODE_CHUNK):
        at = pl.ds(i * NODE_CHUNK, NODE_CHUNK)
        rtab[at, :] = mm(node_ref[at, :], w_r).astype(BF16)

    iota_r[...] = lax.broadcasted_iota(jnp.int32, (16, WINDOW), 1).astype(jnp.int16)
    iota_c[...] = lax.broadcasted_iota(jnp.int32, (WINDOW, LANES), 0).astype(jnp.int16)
    rtab[pl.ds(NODES, WINDOW), :] = jnp.zeros((WINDOW, D), BF16)
    agtab[pl.ds(NODES, WINDOW), :] = jnp.zeros((WINDOW, D), BF16)
    agg[...] = jnp.zeros_like(agg)
    frecv[...] = jnp.zeros_like(frecv)
    for ref in (wge, wgm, wgo, wni, wnm, wno):
        ref[...] = jnp.zeros_like(ref)

    def window_of(b):
        start = pl.multiple_of((recv_sm[b * ROWS, 0] // 16) * 16, 16)
        windows = (recv_sm[b * ROWS + ROWS - 1, LANES - 1] - start) // WINDOW + 1
        return start, windows

    def tile_hot(col16, width):
        tiles = []
        for r in range(LANES // 16):
            part = col16[r * 16 : r * 16 + 16]
            tiles.append(
                jnp.concatenate(
                    [
                        hot(part == iota_r[:, t * LANES : (t + 1) * LANES])
                        for t in range(width // LANES)
                    ],
                    axis=1,
                )
            )
        return jnp.concatenate(tiles, axis=0)

    def row_hot(row, height):
        row16 = jnp.broadcast_to(row, (16, LANES)).astype(jnp.int16)
        return jnp.concatenate(
            [hot(row16 == iota_c[k * 16 : k * 16 + 16, :]) for k in range(height // 16)], axis=0
        )

    def receiver_hot(b, start, extra):
        parts = []
        for r in range(ROWS):
            row = recv_ref[pl.ds(b * ROWS + r, 1), :] - start
            place = b * BLOCK + r * LANES + lax.broadcasted_iota(jnp.int32, (1, LANES), 1)
            row = jnp.where((place < count) & (row >= 0) & (row < WINDOW), row, -1)
            parts.append(row_hot(row, WINDOW))
        return jnp.concatenate(parts, axis=1)

    def column_hot_windows(col, start, k):
        local = col - (start + k * WINDOW)
        local = jnp.where((local >= 0) & (local < WINDOW), local, -1).astype(jnp.int16)
        return tile_hot(local, WINDOW)

    def forward_block(b, single):
        start, windows = window_of(b)
        for c in range(CHUNKS):
            at = pl.ds(b * BLOCK + c * CHUNK, CHUNK)
            recv_cols = []
            for r in range(CHUNK // LANES):
                line = pl.ds(b * ROWS + c * (CHUNK // LANES) + r, 1)
                recv_cols.append(columns_of(recv_ref[line, :]))
            pre = mm(jnp.concatenate([edge_v[at, :], picked_v[at, :]], axis=1), w_es)
            if single:
                near = jnp.concatenate([column_hot_windows(x, start, 0) for x in recv_cols], axis=0)
                hotr[at, :] = near
                pre = pre + mm(near, rtab[pl.ds(start, WINDOW), :])
            else:

                def add(k, total):
                    near = jnp.concatenate(
                        [column_hot_windows(x, start, k) for x in recv_cols], axis=0
                    )
                    place = pl.multiple_of(start + k * WINDOW, 16)
                    return total + mm(near, rtab[pl.ds(place, WINDOW), :])

                pre = lax.fori_loop(0, windows, add, pre)
            act1, slope1 = silu_pair(pre)
            a1[at, :] = act1
            d1[at, :] = slope1
            act2, slope2 = silu_pair(mm(act1, ewm_ref[...]))
            a2[at, :] = act2
            d2[at, :] = slope2
            normed, inverse = normalise(mm(act2, ewo_ref[...]))
            nrm[at, :] = normed.astype(BF16)
            inv[at, :] = jnp.broadcast_to(inverse, (CHUNK, D)).astype(BF16)
        rows = pl.ds(b * BLOCK, BLOCK)

        def send_on(k, carry):
            place = pl.multiple_of(start + k * WINDOW, 16)
            into = pl.ds(place, WINDOW)
            agg[into, :] += mm(receiver_hot(b, place, None), nrm[rows, :])
            return carry

        if single:
            send_on(0, 0)
        else:
            lax.fori_loop(0, windows, send_on, 0)

    @pl.loop(0, BLOCKS)
    def _(b):
        block_copy(edge_hbm, edge_v, sem_e, b).wait()
        block_copy(picked_hbm, picked_v, sem_p, b).wait()
        windows = window_of(b)[1]
        live = b * BLOCK < count

        @pl.when(live & (windows == 1))
        def _():
            forward_block(b, True)

        @pl.when(live & (windows > 1))
        def _():
            forward_block(b, False)

    @pl.loop(0, NODES // NODE_CHUNK)
    def _(i):
        at = pl.ds(i * NODE_CHUNK, NODE_CHUNK)
        own = node_ref[at, :]
        total = agg[at, :].astype(BF16)
        inputs = jnp.concatenate([own, total], axis=1)
        act1, slope1 = silu_pair(mm(inputs, nwi_ref[...]))
        act2, slope2 = silu_pair(mm(act1, nwm_ref[...]))
        normed, inverse = normalise(mm(act2, nwo_ref[...]))
        g = ncot_ref[at, :].astype(F32)
        top = norm_grad(g, normed, inverse).astype(BF16)
        wno[...] += t_mm(act2, top)
        second = (mm_t(top, nwo_ref[...]) * slope2.astype(F32)).astype(BF16)
        wnm[...] += t_mm(act1, second)
        first = (mm_t(second, nwm_ref[...]) * slope1.astype(F32)).astype(BF16)
        wni[...] += t_mm(inputs, first)
        back = mm_t(first, nwi_ref[...])
        own_ref[at, :] = g + back[:, :D]
        agtab[at, :] = back[:, D:].astype(BF16)

    def backward_block(b, single):
        start, windows = window_of(b)
        for c in range(CHUNKS):
            at = pl.ds(b * BLOCK + c * CHUNK, CHUNK)
            here = pl.ds(c * CHUNK, CHUNK)
            cot = cot_v[at, :].astype(F32)
            if single:
                g = cot + mm(hotr[at, :], agtab[pl.ds(start, WINDOW), :])
            else:
                cols = []
                for r in range(CHUNK // LANES):
                    line = pl.ds(b * ROWS + c * (CHUNK // LANES) + r, 1)
                    cols.append(columns_of(recv_ref[line, :]))

                def add(k, total):
                    near = jnp.concatenate([column_hot_windows(x, start, k) for x in cols], axis=0)
                    place = pl.multiple_of(start + k * WINDOW, 16)
                    return total + mm(near, agtab[pl.ds(place, WINDOW), :])

                g = lax.fori_loop(0, windows, add, cot)
            place = b * BLOCK + c * CHUNK + lax.broadcasted_iota(jnp.int32, (CHUNK, D), 0)
            live = place < count
            top = norm_grad(g, nrm[at, :].astype(F32), inv[at, :].astype(F32))
            top = jnp.where(live, top, 0.0).astype(BF16)
            tgs[here, :] = top
            second = (mm_t(top, ewo_ref[...]) * d2[at, :].astype(F32)).astype(BF16)
            sgs[here, :] = second
            first = (mm_t(second, ewm_ref[...]) * d1[at, :].astype(F32)).astype(BF16)
            first_v[at, :] = first
            grad = cot + mm_t(first, w_e)
            cot_v[at, :] = jnp.where(live, grad, 0.0).astype(BF16)
        out_copy(b).start()
        first_copy(b).start()
        rows = pl.ds(b * BLOCK, BLOCK)
        wgo[...] += t_mm(a2[rows, :], tgs[...])
        wgm[...] += t_mm(a1[rows, :], sgs[...])
        wge[0:D, :] += t_mm(edge_v[rows, :], first_v[rows, :])
        wge[D : 2 * D, :] += t_mm(picked_v[rows, :], first_v[rows, :])

        def send_on(k, carry):
            place = pl.multiple_of(start + k * WINDOW, 16)
            into = pl.ds(place, WINDOW)
            frecv[into, :] += mm(receiver_hot(b, place, None), first_v[rows, :])
            return carry

        if single:
            send_on(0, 0)
        else:
            lax.fori_loop(0, windows, send_on, 0)

    @pl.loop(0, BLOCKS)
    def _(b):
        block_copy(cot_hbm, cot_v, sem_c, b).wait()
        windows = window_of(b)[1]
        live = b * BLOCK < count

        @pl.when(live & (windows == 1))
        def _():
            backward_block(b, True)

        @pl.when(live & (windows > 1))
        def _():
            backward_block(b, False)

        @pl.when(jnp.logical_not(live))
        def _():
            cot_v[pl.ds(b * BLOCK, BLOCK), :] = jnp.zeros((BLOCK, D), BF16)
            first_v[pl.ds(b * BLOCK, BLOCK), :] = jnp.zeros((BLOCK, D), BF16)
            out_copy(b).start()
            first_copy(b).start()

    wrecv = jnp.zeros((D, D), F32)
    for i in range(NODES // NODE_CHUNK):
        at = pl.ds(i * NODE_CHUNK, NODE_CHUNK)
        recv = frecv[at, :].astype(BF16)
        own_ref[at, :] += mm_t(recv, w_r)
        wrecv = wrecv + t_mm(node_ref[at, :], recv)
    wg_ref[0 : 2 * D, :] = wge[...].astype(BF16)
    wg_ref[2 * D : 3 * D, :] = wrecv.astype(BF16)
    wg_ref[3 * D : 4 * D, :] = wgm[...].astype(BF16)
    wg_ref[4 * D : 5 * D, :] = wgo[...].astype(BF16)
    wg_ref[5 * D : 7 * D, :] = wni[...].astype(BF16)
    wg_ref[7 * D : 8 * D, :] = wnm[...].astype(BF16)
    wg_ref[8 * D : 9 * D, :] = wno[...].astype(BF16)
    wg_ref[9 * D : 10 * D, :] = jnp.zeros((D, D), BF16)

    @pl.loop(0, BLOCKS)
    def _(b):
        out_copy(b).wait()
        first_copy(b).wait()


def partition_call(count, node, ncot, edge, cot, picked, recv, weights):
    vm = pl.BlockSpec(memory_space=pltpu.VMEM)
    sm = pl.BlockSpec(memory_space=pltpu.SMEM)
    hb = pl.BlockSpec(memory_space=pl.ANY)
    v = pltpu.VMEM
    return pl.pallas_call(
        partition_kernel,
        out_shape=(
            jax.ShapeDtypeStruct((EDGES, D), BF16),
            jax.ShapeDtypeStruct((EDGES, D), BF16),
            jax.ShapeDtypeStruct((NODES, D), F32),
            jax.ShapeDtypeStruct((W_ROWS, D), BF16),
        ),
        in_specs=[sm, sm, vm, vm, hb, hb, hb, vm] + [vm] * 6,
        out_specs=(hb, hb, vm, vm),
        scratch_shapes=[
            v((EDGES, D), BF16), v((EDGES, D), BF16), v((EDGES, D), BF16), v((EDGES, D), BF16),
            v((PADDED, D), BF16), v((PADDED, D), F32), v((PADDED, D), BF16), v((PADDED, D), F32),
            v((EDGES, D), BF16), v((EDGES, D), BF16), v((EDGES, D), BF16), v((EDGES, D), BF16),
            v((EDGES, D), BF16), v((EDGES, D), BF16), v((EDGES, WINDOW), BF16),
            v((BLOCK, D), BF16), v((BLOCK, D), BF16),
            v((16, WINDOW), jnp.int16), v((WINDOW, LANES), jnp.int16),
            v((2 * D, D), F32), v((D, D), F32), v((D, D), F32),
            v((2 * D, D), F32), v((D, D), F32), v((D, D), F32),
        ] + [pltpu.SemaphoreType.DMA((BLOCKS,))] * 5,
        compiler_params=pltpu.CompilerParams(vmem_limit_bytes=VMEM_LIMIT),
        name="partition",
    )(count, recv, node, ncot, edge, cot, picked, recv, *weights)


def cell(w, v):
    return {"wide": w, "narrow": v}


def swap_halos(w, v, wide, narrow, blocks, landing, send_sem, recv_sem):
    sides = (
        (w > 0, cell(w - 1, v)),
        (w < wide - 1, cell(w + 1, v)),
        (v > 0, cell(w, v - 1)),
        (v < narrow - 1, cell(w, v + 1)),
    )

    def transfer(j, slot):
        return pltpu.make_async_remote_copy(
            src_ref=blocks.at[pl.ds(j * HALO, HALO), :],
            dst_ref=landing.at[pl.ds(slot * HALO, HALO), :],
            send_sem=send_sem.at[j],
            recv_sem=recv_sem.at[slot],
            device_id=sides[j][1],
            device_id_type=MESH,
        )

    def start(j):
        @pl.when(sides[j][0])
        def _():
            transfer(j, j ^ 1).start()

    def finish(j):
        @pl.when(sides[j][0])
        def _():
            transfer(j, j ^ 1).wait_send()
            transfer(j, j).wait_recv()

        @pl.when(jnp.logical_not(sides[j][0]))
        def _():
            landing[pl.ds(j * HALO, HALO), :] = jnp.zeros((HALO, D), BF16)

    def greet(barrier):
        for there, device in sides:

            @pl.when(there)
            def _():
                pl.semaphore_signal(barrier, inc=1, device_id=device, device_id_type=MESH)

        return sum(there.astype(jnp.int32) for there, _ in sides)

    return greet, start, finish


def column_hot(cols, iota, width):
    return jnp.concatenate(
        [hot(cols == iota[:, t * LANES : (t + 1) * LANES]) for t in range(width // LANES)], axis=1
    )


def gather_kernel(
    wide, narrow, node_ref, out_rows_ref, send_ref, picked_hbm,
    outgoing, landing, table, iota_ref, held, send_sem, recv_sem, out_sem,
):
    w, v = lax.axis_index("wide"), lax.axis_index("narrow")
    greet, start, finish = swap_halos(w, v, wide, narrow, outgoing, landing, send_sem, recv_sem)
    barrier = pltpu.get_barrier_semaphore()
    peers = greet(barrier)
    iota_ref[...] = lax.broadcasted_iota(jnp.int32, (LANES, NODES), 1).astype(jnp.int16)
    half = NODES // 2
    table[0:half, 0:D] = node_ref[0:half, :]
    table[0:half, D : 2 * D] = node_ref[half:NODES, :]

    for j in range(4):
        hots, high = [], []
        for c in range(HALO // LANES):
            col = columns_of(out_rows_ref[j : j + 1, c * LANES : (c + 1) * LANES])
            high.append(col >= half)
            hots.append(column_hot((col & (half - 1)).astype(jnp.int16), iota_ref, half))
        both = mm(jnp.concatenate(hots, axis=0), table[0:half, :])
        rows = jnp.where(jnp.concatenate(high, axis=0), both[:, D:], both[:, :D])
        outgoing[pl.ds(j * HALO, HALO), :] = rows.astype(BF16)
        if j == 0:
            pl.semaphore_wait(barrier, peers)
        start(j)

    def out_copy(b):
        at = pl.ds(b * BLOCK, BLOCK)
        return pltpu.make_async_copy(held.at[at, :], picked_hbm.at[at, :], out_sem.at[b])

    def pick(b, own, far):
        hots, high = [], []
        for r in range(ROWS):
            col = columns_of(send_ref[pl.ds(b * ROWS + r, 1), :])
            high.append((col & half) != 0)
            place = (col & (half - 1)) + jnp.where(col >= NODES, half, 0)
            if not own:
                place = place - half
            hots.append(column_hot(place.astype(jnp.int16), iota_ref, half * (own + far)))
        lower = 0 if own else half
        both = mm(jnp.concatenate(hots, axis=0), table[lower : lower + half * (own + far), :])
        return jnp.where(jnp.concatenate(high, axis=0), both[:, D:], both[:, :D]).astype(BF16)

    @pl.loop(0, EARLY)
    def _(b):
        held[pl.ds(b * BLOCK, BLOCK), :] = pick(b, True, False)

    for j in range(4):
        finish(j)
    table[half:NODES, 0:D] = landing[0:half, :]
    table[half:NODES, D : 2 * D] = landing[half:NODES, :]

    @pl.loop(0, EARLY)
    def _(b):
        held[pl.ds(b * BLOCK, BLOCK), :] += pick(b, False, True)
        out_copy(b).start()

    @pl.loop(EARLY, BLOCKS)
    def _(b):
        held[pl.ds(b * BLOCK, BLOCK), :] = pick(b, True, True)
        out_copy(b).start()

    @pl.loop(0, BLOCKS)
    def _(b):
        out_copy(b).wait()


def gather_call(wide, narrow, node, out_rows, send):
    vm = pl.BlockSpec(memory_space=pltpu.VMEM)
    sem = pltpu.SemaphoreType.DMA
    return pl.pallas_call(
        functools.partial(gather_kernel, wide, narrow),
        out_shape=jax.ShapeDtypeStruct((EDGES, D), BF16),
        in_specs=[vm, vm, vm],
        out_specs=pl.BlockSpec(memory_space=pl.ANY),
        scratch_shapes=[
            pltpu.VMEM((4 * HALO, D), BF16),
            pltpu.VMEM((4 * HALO, D), BF16),
            pltpu.VMEM((NODES, 2 * D), BF16),
            pltpu.VMEM((LANES, NODES), jnp.int16),
            pltpu.VMEM((EDGES, D), BF16),
            sem((4,)), sem((4,)), sem((BLOCKS,)),
        ],
        compiler_params=pltpu.CompilerParams(
            collective_id=0, has_side_effects=True, vmem_limit_bytes=VMEM_LIMIT
        ),
        name="gather",
    )(node, out_rows, send)


def scatter_kernel(
    wide, narrow, first_hbm, send_ref, own_ref, wg_ref, ewi_ref, out_rows_ref, node_ref, sum_ref,
    first_v, f2, iota_c, border, landing, pair, half, quarter, part, along_z, other, along_x, third,
    first_sem, send_h, recv_h, send_a, recv_a,
):
    w, v = lax.axis_index("wide"), lax.axis_index("narrow")
    y, zh, core = w // 4, (w // 2) % 2, w % 2
    x, zl = v // 2, v % 2
    z = zh * 2 + zl
    n_half, n_quarter = W_ROWS // 2, W_ROWS // 8

    def block_copy(b):
        at = pl.ds(b * BLOCK, BLOCK)
        return pltpu.make_async_copy(first_hbm.at[at, :], first_v.at[at, :], first_sem.at[b])

    @pl.loop(0, BLOCKS)
    def _(b):
        block_copy(b).start()

    greet, start, finish = swap_halos(w, v, wide, narrow, border, landing, send_h, recv_h)

    def rank(y, zh, core, x, zl):
        return cell(y * 4 + zh * 2 + core, x * 2 + zl)

    partner = rank(y, zh, 1 - core, x, zl)
    y_peers = [((y + i) % 4, rank((y + i) % 4, zh, core, x, zl)) for i in range(1, 4)]
    z_peers = [rank(y, (zh + i) % 2, core, x, (zl + j) % 2) for i, j in ((0, 1), (1, 0), (1, 1))]
    x_peers = [rank(y, zh, core, (x + i) % 4, zl) for i in range(1, 4)]
    barrier = pltpu.get_barrier_semaphore()
    peers = greet(barrier)
    others = [partner] + [d for _, d in y_peers] + z_peers + x_peers
    for device in others:
        pl.semaphore_signal(barrier, inc=1, device_id=device, device_id_type=MESH)

    iota_c[...] = lax.broadcasted_iota(jnp.int32, (NODES, LANES), 0).astype(jnp.int16)
    f2[...] = jnp.zeros_like(f2)
    pl.semaphore_wait(barrier, peers + len(others))

    def send(i, src, dst, device):
        return pltpu.make_async_remote_copy(
            src_ref=src, dst_ref=dst, send_sem=send_a.at[i], recv_sem=recv_a.at[i], device_id=device,
            device_id_type=MESH,
        )

    def half_rows(i):
        return pl.ds(pl.multiple_of(i * n_half, 16), n_half)

    def quarter_rows(i):
        return pl.ds(pl.multiple_of(i * n_quarter, 16), n_quarter)

    def mine():
        return pl.ds(pl.multiple_of(core * n_half + y * n_quarter, 16), n_quarter)

    def scatter(lo, hi):
        @pl.loop(lo, hi)
        def _(b):
            block_copy(b).wait()
            rows = pl.ds(b * BLOCK, BLOCK)
            value = first_v[rows, :]
            far, hots = [], []
            for r in range(ROWS):
                line = send_ref[pl.ds(b * ROWS + r, 1), :]
                far.append(hot(columns_of(line) >= NODES))
                line16 = jnp.broadcast_to(line & (NODES - 1), (16, LANES)).astype(jnp.int16)
                hots.append(
                    jnp.concatenate(
                        [hot(line16 == iota_c[k * 16 : k * 16 + 16, :]) for k in range(NODES // 16)],
                        axis=0,
                    )
                )
            away = value * jnp.concatenate(far, axis=0)
            f2[...] += mm(
                jnp.concatenate(hots, axis=1), jnp.concatenate([value - away, away], axis=1)
            )

    def total_of(ref):
        total = ref[0].astype(F32)
        for i in range(1, 4):
            total = total + ref[i].astype(F32)
        return total.astype(BF16)

    stage = [send(0, wg_ref.at[half_rows(1 - core), :], pair, partner)]
    started = list(stage)
    stage[0].start()
    scatter(0, 2)
    stage[0].wait_recv()
    half[...] = (wg_ref[half_rows(core), :].astype(F32) + pair[...].astype(F32)).astype(BF16)
    stage = [
        send(i, half.at[quarter_rows(to), :], quarter.at[i], device)
        for i, (to, device) in enumerate(y_peers, 1)
    ]
    for c in stage:
        c.start()
    started += stage
    scatter(2, 5)
    for c in stage:
        c.wait_recv()
    quarter[0] = half[quarter_rows(y), :]
    part[...] = total_of(quarter)
    stage = [send(i, part, along_z.at[z], device) for i, device in enumerate(z_peers, 4)]
    for c in stage:
        c.start()
    started += stage
    along_z[z] = part[...]
    scatter(5, 8)
    for c in stage:
        c.wait_recv()
    other[...] = total_of(along_z)
    stage = [send(i, other, along_x.at[x], device) for i, device in enumerate(x_peers, 7)]
    for c in stage:
        c.start()
    started += stage
    along_x[x] = other[...]
    scatter(8, 11)
    for c in stage:
        c.wait_recv()
    third[mine(), :] = total_of(along_x)
    stage = [
        send(i, third.at[mine(), :], third.at[mine(), :], device)
        for i, (_, device) in enumerate(y_peers, 10)
    ]
    for c in stage:
        c.start()
    started += stage
    scatter(11, BLOCKS)

    w_s = ewi_ref[D : 2 * D]
    border[...] = mm_t(f2[:, D : 2 * D].astype(BF16), w_s).astype(BF16)
    for j in range(4):
        start(j)
    for c in stage:
        c.wait_recv()
    stage = [send(13, third.at[half_rows(core), :], third.at[half_rows(core), :], partner)]
    stage[0].start()
    started += stage
    near = mm_t(f2[:, 0:D].astype(BF16), w_s)
    for j in range(4):
        finish(j)
    hots = []
    for j in range(4):
        for c in range(HALO // LANES):
            line = out_rows_ref[j : j + 1, c * LANES : (c + 1) * LANES]
            line16 = jnp.broadcast_to(line, (16, LANES)).astype(jnp.int16)
            hots.append(
                jnp.concatenate(
                    [hot(line16 == iota_c[k * 16 : k * 16 + 16, :]) for k in range(NODES // 16)],
                    axis=0,
                )
            )
    node_ref[...] = own_ref[...] + near + mm(jnp.concatenate(hots, axis=1), landing[...])
    stage[0].wait_recv()
    sum_ref[...] = third[...]
    for c in started:
        c.wait_send()


def scatter_call(wide, narrow, first, send, own, wg, ewi, out_rows):
    vm = pl.BlockSpec(memory_space=pltpu.VMEM)
    v = pltpu.VMEM
    sem = pltpu.SemaphoreType.DMA
    quarter = W_ROWS // 8
    return pl.pallas_call(
        functools.partial(scatter_kernel, wide, narrow),
        out_shape=(
            jax.ShapeDtypeStruct((NODES, D), F32),
            jax.ShapeDtypeStruct((W_ROWS, D), BF16),
        ),
        in_specs=[pl.BlockSpec(memory_space=pl.ANY)] + [vm] * 5,
        out_specs=(vm, vm),
        scratch_shapes=[
            v((EDGES, D), BF16), v((NODES, 2 * D), F32), v((NODES, LANES), jnp.int16),
            v((4 * HALO, D), BF16), v((4 * HALO, D), BF16),
            v((W_ROWS // 2, D), BF16), v((W_ROWS // 2, D), BF16), v((4, quarter, D), BF16),
            v((quarter, D), BF16), v((4, quarter, D), BF16), v((quarter, D), BF16),
            v((4, quarter, D), BF16), v((W_ROWS, D), BF16),
            sem((BLOCKS,)), sem((4,)), sem((4,)), sem((14,)), sem((14,)),
        ],
        compiler_params=pltpu.CompilerParams(
            collective_id=1, has_side_effects=True, vmem_limit_bytes=VMEM_LIMIT
        ),
        name="scatter",
    )(first, send, own, wg, ewi, out_rows)


def unpack_kernel(scales, sum_ref, *outs):
    at = 0
    for out, scale in zip(outs, scales):
        rows = out.shape[0]
        out[...] = sum_ref[at : at + rows, :].astype(F32) * scale
        at += rows


def unpack_call(scales, summed, shapes):
    vm = pl.BlockSpec(memory_space=pltpu.VMEM)
    return pl.pallas_call(
        functools.partial(unpack_kernel, scales),
        out_shape=tuple(jax.ShapeDtypeStruct(s, F32) for s in shapes),
        in_specs=[vm],
        out_specs=(vm,) * 6,
        name="unpack",
    )(summed)


def per_device(
    wide,
    narrow,
    node_hidden_state,
    edge_hidden_state,
    node_output_gradient,
    edge_output_gradient,
    senders,
    receivers,
    edge_slot_count,
    outbound_rows,
    *weights,
):
    out_rows = outbound_rows.reshape(4, HALO)
    send = senders.reshape(EDGES // LANES, LANES)
    recv = receivers.reshape(EDGES // LANES, LANES)
    picked = gather_call(wide, narrow, node_hidden_state, out_rows, send)
    edge_grad, first, own, wg = partition_call(
        edge_slot_count,
        node_hidden_state,
        node_output_gradient,
        edge_hidden_state,
        edge_output_gradient,
        picked,
        recv,
        weights,
    )
    node_grad, summed = scatter_call(wide, narrow, first, send, own, wg, weights[0], out_rows)
    edge_scale = 1.0 / math.sqrt(EDGES * wide * narrow)
    node_scale = 1.0 / math.sqrt(NODES * wide * narrow)
    sums = unpack_call((edge_scale,) * 3 + (node_scale,) * 3, summed, [x.shape for x in weights])
    return (node_grad, edge_grad, *sums)


def solution(mesh):
    both = ("wide", "narrow")
    rows, flat = P(both, None), P(both)
    return jax.shard_map(
        functools.partial(per_device, mesh.shape["wide"], mesh.shape["narrow"]),
        mesh=mesh,
        in_specs=(rows, rows, rows, rows, flat, flat, flat, P(both, None, None)) + (P(),) * 6,
        out_specs=(rows, rows) + (P(),) * 6,
        check_vma=False,
    )
```

```python
import functools
import math

import jax
import jax.numpy as jnp
from jax import lax
from jax.experimental import pallas as pl
from jax.experimental.pallas import tpu as pltpu
from jax.sharding import PartitionSpec as P

F32 = jnp.float32
BF16 = jnp.bfloat16
MESH = pl.DeviceIdType.MESH
EPS = 1e-05

D = 128
NODES = 2048
HALO = 512
EDGES = 12288
BLOCK = 1024
CHUNK = 1024
NODE_CHUNK = 1024
BLOCKS = EDGES // BLOCK
CHUNKS = BLOCK // CHUNK
WINDOW = 256
LANES = 128
ROWS = BLOCK // LANES
PADDED = NODES + WINDOW
W_ROWS = 1280
STEP = 2048
STEPS = EDGES // STEP
STEP_ROWS = STEP // LANES
EARLY = 6
VMEM_LIMIT = 62 * 1024 * 1024


def mm(a, b):
    return jnp.dot(a, b, preferred_element_type=F32)


def mm_t(a, b):
    return lax.dot_general(a, b, (((1,), (1,)), ((), ())), preferred_element_type=F32)


def t_mm(a, b):
    return lax.dot_general(a, b, (((0,), (0,)), ((), ())), preferred_element_type=F32)


def silu_pair(v):
    s = 0.5 * jnp.tanh(0.5 * v) + 0.5
    a = v * s
    return a.astype(BF16), (s + a * (1.0 - s)).astype(BF16)


def centre_columns(weight):
    wide = weight.astype(F32)
    return (wide - jnp.mean(wide, axis=-1, keepdims=True)).astype(BF16)


def normalise(centred):
    inverse = lax.rsqrt(jnp.mean(centred * centred, axis=-1, keepdims=True) + EPS)
    return centred * inverse, inverse


def norm_grad(g, normed, inverse):
    return inverse * (
        g
        - jnp.mean(g, axis=-1, keepdims=True)
        - normed * jnp.mean(g * normed, axis=-1, keepdims=True)
    )


def columns_of(row):
    return jnp.transpose(jnp.broadcast_to(row, (LANES, LANES)))


def hot(mask):
    return jnp.where(mask, jnp.ones((), BF16), jnp.zeros((), BF16))


def partition_kernel(
    count_ref, recv_sm, node_ref, ncot_ref, edge_hbm, cot_hbm, picked_hbm, recv_ref,
    ewi_ref, ewm_ref, ewo_ref, nwi_ref, nwm_ref, nwo_ref,
    egrad_hbm, first_hbm, own_ref, wg_ref,
    edge_v, cot_v, picked_v, first_v, rtab, agg, agtab, frecv, a1, d1, a2, d2, nrm, inv, hotr,
    tgs, sgs, iota_r, iota_c, wge, wgm, wgo, wni, wnm, wno, sem_e, sem_c, sem_p, sem_g, sem_f,
):
    count = count_ref[0]

    def block_copy(hbm, v, sem, b):
        at = pl.ds(b * BLOCK, BLOCK)
        return pltpu.make_async_copy(hbm.at[at, :], v.at[at, :], sem.at[b])

    def out_copy(b):
        at = pl.ds(b * BLOCK, BLOCK)
        return pltpu.make_async_copy(cot_v.at[at, :], egrad_hbm.at[at, :], sem_g.at[b])

    def first_copy(b):
        at = pl.ds(b * BLOCK, BLOCK)
        return pltpu.make_async_copy(first_v.at[at, :], first_hbm.at[at, :], sem_f.at[b])

    @pl.loop(0, BLOCKS)
    def _(b):
        block_copy(edge_hbm, edge_v, sem_e, b).start()
        block_copy(picked_hbm, picked_v, sem_p, b).start()

    @pl.loop(0, BLOCKS)
    def _(b):
        block_copy(cot_hbm, cot_v, sem_c, b).start()

    ewo_c, nwo_c = centre_columns(ewo_ref[...]), centre_columns(nwo_ref[...])
    w_e, w_es, w_r = ewi_ref[0:D], ewi_ref[0 : 2 * D], ewi_ref[2 * D : 3 * D]

    for i in range(NODES // NODE_CHUNK):
        at = pl.ds(i * NODE_CHUNK, NODE_CHUNK)
        rtab[at, :] = mm(node_ref[at, :], w_r).astype(BF16)

    iota_r[...] = lax.broadcasted_iota(jnp.int32, (16, WINDOW), 1).astype(jnp.int16)
    iota_c[...] = lax.broadcasted_iota(jnp.int32, (WINDOW, LANES), 0).astype(jnp.int16)
    rtab[pl.ds(NODES, WINDOW), :] = jnp.zeros((WINDOW, D), BF16)
    agtab[pl.ds(NODES, WINDOW), :] = jnp.zeros((WINDOW, D), BF16)
    agg[...] = jnp.zeros_like(agg)
    frecv[...] = jnp.zeros_like(frecv)
    for ref in (wge, wgm, wgo, wni, wnm, wno):
        ref[...] = jnp.zeros_like(ref)

    def window_of(b):
        start = pl.multiple_of((recv_sm[b * ROWS, 0] // 16) * 16, 16)
        windows = (recv_sm[b * ROWS + ROWS - 1, LANES - 1] - start) // WINDOW + 1
        return start, windows

    def tile_hot(col16, width):
        tiles = []
        for r in range(LANES // 16):
            part = col16[r * 16 : r * 16 + 16]
            tiles.append(
                jnp.concatenate(
                    [
                        hot(part == iota_r[:, t * LANES : (t + 1) * LANES])
                        for t in range(width // LANES)
                    ],
                    axis=1,
                )
            )
        return jnp.concatenate(tiles, axis=0)

    def row_hot(row, height):
        row16 = jnp.broadcast_to(row, (16, LANES)).astype(jnp.int16)
        return jnp.concatenate(
            [hot(row16 == iota_c[k * 16 : k * 16 + 16, :]) for k in range(height // 16)], axis=0
        )

    def receiver_hot(b, start, extra):
        parts = []
        for r in range(ROWS):
            row = recv_ref[pl.ds(b * ROWS + r, 1), :] - start
            place = b * BLOCK + r * LANES + lax.broadcasted_iota(jnp.int32, (1, LANES), 1)
            row = jnp.where((place < count) & (row >= 0) & (row < WINDOW), row, -1)
            parts.append(row_hot(row, WINDOW))
        return jnp.concatenate(parts, axis=1)

    def column_hot_windows(col, start, k):
        local = col - (start + k * WINDOW)
        local = jnp.where((local >= 0) & (local < WINDOW), local, -1).astype(jnp.int16)
        return tile_hot(local, WINDOW)

    def forward_block(b, single):
        start, windows = window_of(b)
        for c in range(CHUNKS):
            at = pl.ds(b * BLOCK + c * CHUNK, CHUNK)
            recv_cols = []
            for r in range(CHUNK // LANES):
                line = pl.ds(b * ROWS + c * (CHUNK // LANES) + r, 1)
                recv_cols.append(columns_of(recv_ref[line, :]))
            pre = mm(jnp.concatenate([edge_v[at, :], picked_v[at, :]], axis=1), w_es)
            if single:
                near = jnp.concatenate([column_hot_windows(x, start, 0) for x in recv_cols], axis=0)
                hotr[at, :] = near
                pre = pre + mm(near, rtab[pl.ds(start, WINDOW), :])
            else:

                def add(k, total):
                    near = jnp.concatenate(
                        [column_hot_windows(x, start, k) for x in recv_cols], axis=0
                    )
                    place = pl.multiple_of(start + k * WINDOW, 16)
                    return total + mm(near, rtab[pl.ds(place, WINDOW), :])

                pre = lax.fori_loop(0, windows, add, pre)
            act1, slope1 = silu_pair(pre)
            a1[at, :] = act1
            d1[at, :] = slope1
            act2, slope2 = silu_pair(mm(act1, ewm_ref[...]))
            a2[at, :] = act2
            d2[at, :] = slope2
            normed, inverse = normalise(mm(act2, ewo_c))
            nrm[at, :] = normed.astype(BF16)
            inv[at, :] = jnp.broadcast_to(inverse, (CHUNK, D)).astype(BF16)
        rows = pl.ds(b * BLOCK, BLOCK)

        def send_on(k, carry):
            place = pl.multiple_of(start + k * WINDOW, 16)
            into = pl.ds(place, WINDOW)
            agg[into, :] += mm(receiver_hot(b, place, None), nrm[rows, :])
            return carry

        if single:
            send_on(0, 0)
        else:
            lax.fori_loop(0, windows, send_on, 0)

    @pl.loop(0, BLOCKS)
    def _(b):
        block_copy(edge_hbm, edge_v, sem_e, b).wait()
        block_copy(picked_hbm, picked_v, sem_p, b).wait()
        windows = window_of(b)[1]
        live = b * BLOCK < count

        @pl.when(live & (windows == 1))
        def _():
            forward_block(b, True)

        @pl.when(live & (windows > 1))
        def _():
            forward_block(b, False)

    @pl.loop(0, NODES // NODE_CHUNK)
    def _(i):
        at = pl.ds(i * NODE_CHUNK, NODE_CHUNK)
        own = node_ref[at, :]
        total = agg[at, :].astype(BF16)
        inputs = jnp.concatenate([own, total], axis=1)
        act1, slope1 = silu_pair(mm(inputs, nwi_ref[...]))
        act2, slope2 = silu_pair(mm(act1, nwm_ref[...]))
        normed, inverse = normalise(mm(act2, nwo_c))
        g = ncot_ref[at, :].astype(F32)
        top = norm_grad(g, normed, inverse).astype(BF16)
        wno[...] += t_mm(act2, top)
        second = (mm_t(top, nwo_ref[...]) * slope2.astype(F32)).astype(BF16)
        wnm[...] += t_mm(act1, second)
        first = (mm_t(second, nwm_ref[...]) * slope1.astype(F32)).astype(BF16)
        wni[...] += t_mm(inputs, first)
        back = mm_t(first, nwi_ref[...])
        own_ref[at, :] = g + back[:, :D]
        agtab[at, :] = back[:, D:].astype(BF16)

    def backward_block(b, single):
        start, windows = window_of(b)
        for c in range(CHUNKS):
            at = pl.ds(b * BLOCK + c * CHUNK, CHUNK)
            here = pl.ds(c * CHUNK, CHUNK)
            cot = cot_v[at, :].astype(F32)
            if single:
                g = cot + mm(hotr[at, :], agtab[pl.ds(start, WINDOW), :])
            else:
                cols = []
                for r in range(CHUNK // LANES):
                    line = pl.ds(b * ROWS + c * (CHUNK // LANES) + r, 1)
                    cols.append(columns_of(recv_ref[line, :]))

                def add(k, total):
                    near = jnp.concatenate([column_hot_windows(x, start, k) for x in cols], axis=0)
                    place = pl.multiple_of(start + k * WINDOW, 16)
                    return total + mm(near, agtab[pl.ds(place, WINDOW), :])

                g = lax.fori_loop(0, windows, add, cot)
            place = b * BLOCK + c * CHUNK + lax.broadcasted_iota(jnp.int32, (CHUNK, D), 0)
            live = place < count
            top = norm_grad(g, nrm[at, :].astype(F32), inv[at, :].astype(F32))
            top = jnp.where(live, top, 0.0).astype(BF16)
            tgs[here, :] = top
            second = (mm_t(top, ewo_ref[...]) * d2[at, :].astype(F32)).astype(BF16)
            sgs[here, :] = second
            first = (mm_t(second, ewm_ref[...]) * d1[at, :].astype(F32)).astype(BF16)
            first_v[at, :] = first
            grad = cot + mm_t(first, w_e)
            cot_v[at, :] = jnp.where(live, grad, 0.0).astype(BF16)
        out_copy(b).start()
        first_copy(b).start()
        rows = pl.ds(b * BLOCK, BLOCK)
        wgo[...] += t_mm(a2[rows, :], tgs[...])
        wgm[...] += t_mm(a1[rows, :], sgs[...])
        wge[0:D, :] += t_mm(edge_v[rows, :], first_v[rows, :])
        wge[D : 2 * D, :] += t_mm(picked_v[rows, :], first_v[rows, :])

        def send_on(k, carry):
            place = pl.multiple_of(start + k * WINDOW, 16)
            into = pl.ds(place, WINDOW)
            frecv[into, :] += mm(receiver_hot(b, place, None), first_v[rows, :])
            return carry

        if single:
            send_on(0, 0)
        else:
            lax.fori_loop(0, windows, send_on, 0)

    @pl.loop(0, BLOCKS)
    def _(b):
        block_copy(cot_hbm, cot_v, sem_c, b).wait()
        windows = window_of(b)[1]
        live = b * BLOCK < count

        @pl.when(live & (windows == 1))
        def _():
            backward_block(b, True)

        @pl.when(live & (windows > 1))
        def _():
            backward_block(b, False)

        @pl.when(jnp.logical_not(live))
        def _():
            cot_v[pl.ds(b * BLOCK, BLOCK), :] = jnp.zeros((BLOCK, D), BF16)
            first_v[pl.ds(b * BLOCK, BLOCK), :] = jnp.zeros((BLOCK, D), BF16)
            out_copy(b).start()
            first_copy(b).start()

    wrecv = jnp.zeros((D, D), F32)
    for i in range(NODES // NODE_CHUNK):
        at = pl.ds(i * NODE_CHUNK, NODE_CHUNK)
        recv = frecv[at, :].astype(BF16)
        own_ref[at, :] += mm_t(recv, w_r)
        wrecv = wrecv + t_mm(node_ref[at, :], recv)
    wg_ref[0 : 2 * D, :] = wge[...].astype(BF16)
    wg_ref[2 * D : 3 * D, :] = wrecv.astype(BF16)
    wg_ref[3 * D : 4 * D, :] = wgm[...].astype(BF16)
    wg_ref[4 * D : 5 * D, :] = wgo[...].astype(BF16)
    wg_ref[5 * D : 7 * D, :] = wni[...].astype(BF16)
    wg_ref[7 * D : 8 * D, :] = wnm[...].astype(BF16)
    wg_ref[8 * D : 9 * D, :] = wno[...].astype(BF16)
    wg_ref[9 * D : 10 * D, :] = jnp.zeros((D, D), BF16)

    @pl.loop(0, BLOCKS)
    def _(b):
        out_copy(b).wait()
        first_copy(b).wait()


def partition_call(count, node, ncot, edge, cot, picked, recv, weights):
    vm = pl.BlockSpec(memory_space=pltpu.VMEM)
    sm = pl.BlockSpec(memory_space=pltpu.SMEM)
    hb = pl.BlockSpec(memory_space=pl.ANY)
    v = pltpu.VMEM
    return pl.pallas_call(
        partition_kernel,
        out_shape=(
            jax.ShapeDtypeStruct((EDGES, D), BF16),
            jax.ShapeDtypeStruct((EDGES, D), BF16),
            jax.ShapeDtypeStruct((NODES, D), F32),
            jax.ShapeDtypeStruct((W_ROWS, D), BF16),
        ),
        in_specs=[sm, sm, vm, vm, hb, hb, hb, vm] + [vm] * 6,
        out_specs=(hb, hb, vm, vm),
        scratch_shapes=[
            v((EDGES, D), BF16), v((EDGES, D), BF16), v((EDGES, D), BF16), v((EDGES, D), BF16),
            v((PADDED, D), BF16), v((PADDED, D), F32), v((PADDED, D), BF16), v((PADDED, D), F32),
            v((EDGES, D), BF16), v((EDGES, D), BF16), v((EDGES, D), BF16), v((EDGES, D), BF16),
            v((EDGES, D), BF16), v((EDGES, D), BF16), v((EDGES, WINDOW), BF16),
            v((BLOCK, D), BF16), v((BLOCK, D), BF16),
            v((16, WINDOW), jnp.int16), v((WINDOW, LANES), jnp.int16),
            v((2 * D, D), F32), v((D, D), F32), v((D, D), F32),
            v((2 * D, D), F32), v((D, D), F32), v((D, D), F32),
        ] + [pltpu.SemaphoreType.DMA((BLOCKS,))] * 5,
        compiler_params=pltpu.CompilerParams(vmem_limit_bytes=VMEM_LIMIT),
        name="partition",
    )(count, recv, node, ncot, edge, cot, picked, recv, *weights)


def cell(w, v):
    return {"wide": w, "narrow": v}


def swap_halos(w, v, wide, narrow, blocks, landing, send_sem, recv_sem):
    sides = (
        (w > 0, cell(w - 1, v)),
        (w < wide - 1, cell(w + 1, v)),
        (v > 0, cell(w, v - 1)),
        (v < narrow - 1, cell(w, v + 1)),
    )

    def transfer(j, slot):
        return pltpu.make_async_remote_copy(
            src_ref=blocks.at[pl.ds(j * HALO, HALO), :],
            dst_ref=landing.at[pl.ds(slot * HALO, HALO), :],
            send_sem=send_sem.at[j],
            recv_sem=recv_sem.at[slot],
            device_id=sides[j][1],
            device_id_type=MESH,
        )

    def start(j):
        @pl.when(sides[j][0])
        def _():
            transfer(j, j ^ 1).start()

    def finish(j):
        @pl.when(sides[j][0])
        def _():
            transfer(j, j ^ 1).wait_send()
            transfer(j, j).wait_recv()

        @pl.when(jnp.logical_not(sides[j][0]))
        def _():
            landing[pl.ds(j * HALO, HALO), :] = jnp.zeros((HALO, D), BF16)

    def greet(barrier):
        for there, device in sides:

            @pl.when(there)
            def _():
                pl.semaphore_signal(barrier, inc=1, device_id=device, device_id_type=MESH)

        return sum(there.astype(jnp.int32) for there, _ in sides)

    return greet, start, finish


def column_hot(cols, iota, width):
    return jnp.concatenate(
        [hot(cols == iota[:, t * LANES : (t + 1) * LANES]) for t in range(width // LANES)], axis=1
    )


def gather_kernel(
    wide, narrow, node_ref, out_rows_ref, send_ref, picked_hbm,
    outgoing, landing, table, iota_ref, held, send_sem, recv_sem, out_sem,
):
    w, v = lax.axis_index("wide"), lax.axis_index("narrow")
    greet, start, finish = swap_halos(w, v, wide, narrow, outgoing, landing, send_sem, recv_sem)
    barrier = pltpu.get_barrier_semaphore()
    peers = greet(barrier)
    half = NODES // 2
    iota_ref[...] = lax.broadcasted_iota(jnp.int32, (LANES, half), 1).astype(jnp.int16)
    table[:, 0:D] = node_ref[0:half, :]
    table[:, D : 2 * D] = node_ref[half:NODES, :]

    for j in range(4):
        hots, high = [], []
        for c in range(HALO // LANES):
            col = columns_of(out_rows_ref[j : j + 1, c * LANES : (c + 1) * LANES])
            high.append(col >= half)
            hots.append(column_hot((col & (half - 1)).astype(jnp.int16), iota_ref, half))
        both = mm(jnp.concatenate(hots, axis=0), table[:, 0 : 2 * D])
        rows = jnp.where(jnp.concatenate(high, axis=0), both[:, D:], both[:, :D])
        outgoing[pl.ds(j * HALO, HALO), :] = rows.astype(BF16)
        if j == 0:
            pl.semaphore_wait(barrier, peers)
        start(j)

    def out_copy(b):
        at = pl.ds(b * STEP, STEP)
        return pltpu.make_async_copy(held.at[at, :], picked_hbm.at[at, :], out_sem.at[b])

    def pick(b, own, far):
        hots, high, halo = [], [], []
        for r in range(STEP_ROWS):
            col = columns_of(send_ref[pl.ds(b * STEP_ROWS + r, 1), :])
            high.append((col & half) != 0)
            halo.append(col >= NODES)
            hots.append(column_hot((col & (half - 1)).astype(jnp.int16), iota_ref, half))
        upper, away = jnp.concatenate(high, axis=0), jnp.concatenate(halo, axis=0)
        lanes = slice(0 if own else 2 * D, 4 * D if far else 2 * D)
        found = mm(jnp.concatenate(hots, axis=0), table[:, lanes])

        def side(at):
            return jnp.where(upper, found[:, at + D : at + 2 * D], found[:, at : at + D])

        near_rows = side(0) if own else 0.0
        far_rows = side(2 * D if own else 0) if far else 0.0
        return jnp.where(away, far_rows, near_rows).astype(BF16)

    @pl.loop(0, EARLY)
    def _(b):
        held[pl.ds(b * STEP, STEP), :] = pick(b, True, False)

    for j in range(4):
        finish(j)
    table[:, 2 * D : 3 * D] = landing[0:half, :]
    table[:, 3 * D : 4 * D] = landing[half:NODES, :]

    @pl.loop(0, EARLY)
    def _(b):
        held[pl.ds(b * STEP, STEP), :] += pick(b, False, True)
        out_copy(b).start()

    @pl.loop(EARLY, STEPS)
    def _(b):
        held[pl.ds(b * STEP, STEP), :] = pick(b, True, True)
        out_copy(b).start()

    @pl.loop(0, STEPS)
    def _(b):
        out_copy(b).wait()


def gather_call(wide, narrow, node, out_rows, send):
    vm = pl.BlockSpec(memory_space=pltpu.VMEM)
    sem = pltpu.SemaphoreType.DMA
    return pl.pallas_call(
        functools.partial(gather_kernel, wide, narrow),
        out_shape=jax.ShapeDtypeStruct((EDGES, D), BF16),
        in_specs=[vm, vm, vm],
        out_specs=pl.BlockSpec(memory_space=pl.ANY),
        scratch_shapes=[
            pltpu.VMEM((4 * HALO, D), BF16),
            pltpu.VMEM((4 * HALO, D), BF16),
            pltpu.VMEM((NODES // 2, 4 * D), BF16),
            pltpu.VMEM((LANES, NODES // 2), jnp.int16),
            pltpu.VMEM((EDGES, D), BF16),
            sem((4,)), sem((4,)), sem((STEPS,)),
        ],
        compiler_params=pltpu.CompilerParams(
            collective_id=0, has_side_effects=True, vmem_limit_bytes=VMEM_LIMIT
        ),
        name="gather",
    )(node, out_rows, send)


def scatter_kernel(
    wide, narrow, first_hbm, send_ref, own_ref, wg_ref, ewi_ref, out_rows_ref, node_ref, sum_ref,
    first_v, f2, iota_c, border, landing, pair, half, quarter, part, along_z, other, along_x, third,
    first_sem, send_h, recv_h, send_a, recv_a,
):
    w, v = lax.axis_index("wide"), lax.axis_index("narrow")
    y, zh, core = w // 4, (w // 2) % 2, w % 2
    x, zl = v // 2, v % 2
    z = zh * 2 + zl
    n_half, n_quarter = W_ROWS // 2, W_ROWS // 8

    def block_copy(b):
        at = pl.ds(b * STEP, STEP)
        return pltpu.make_async_copy(first_hbm.at[at, :], first_v.at[at, :], first_sem.at[b])

    @pl.loop(0, STEPS)
    def _(b):
        block_copy(b).start()

    greet, start, finish = swap_halos(w, v, wide, narrow, border, landing, send_h, recv_h)

    def rank(y, zh, core, x, zl):
        return cell(y * 4 + zh * 2 + core, x * 2 + zl)

    partner = rank(y, zh, 1 - core, x, zl)
    y_peers = [((y + i) % 4, rank((y + i) % 4, zh, core, x, zl)) for i in range(1, 4)]
    z_peers = [rank(y, (zh + i) % 2, core, x, (zl + j) % 2) for i, j in ((0, 1), (1, 0), (1, 1))]
    x_peers = [rank(y, zh, core, (x + i) % 4, zl) for i in range(1, 4)]
    barrier = pltpu.get_barrier_semaphore()
    peers = greet(barrier)
    others = [partner] + [d for _, d in y_peers] + z_peers + x_peers
    for device in others:
        pl.semaphore_signal(barrier, inc=1, device_id=device, device_id_type=MESH)

    iota_c[...] = lax.broadcasted_iota(jnp.int32, (NODES, LANES), 0).astype(jnp.int16)
    f2[...] = jnp.zeros_like(f2)

    def send(i, src, dst, device):
        return pltpu.make_async_remote_copy(
            src_ref=src, dst_ref=dst, send_sem=send_a.at[i], recv_sem=recv_a.at[i], device_id=device,
            device_id_type=MESH,
        )

    def half_rows(i):
        return pl.ds(pl.multiple_of(i * n_half, 16), n_half)

    def quarter_rows(i):
        return pl.ds(pl.multiple_of(i * n_quarter, 16), n_quarter)

    def mine():
        return pl.ds(pl.multiple_of(core * n_half + y * n_quarter, 16), n_quarter)

    def scatter(far, lo, hi):
        into = pl.ds(HALO if far else 0, HALO)

        @pl.loop(lo, hi)
        def _(b):
            if far:
                block_copy(b).wait()
            parts, hots = [], []
            for r in range(STEP_ROWS):
                line = send_ref[pl.ds(b * STEP_ROWS + r, 1), :]
                value = first_v[pl.ds(b * STEP + r * LANES, LANES), :]
                group = (columns_of(line) // HALO).astype(jnp.int16)
                parts.append(
                    jnp.concatenate(
                        [
                            jnp.where(group == jnp.int16(4 * far + j), value, jnp.zeros((), BF16))
                            for j in range(4)
                        ],
                        axis=1,
                    )
                )
                hots.append(row_hot(line & (HALO - 1), HALO))
            f2[into, :] += mm(jnp.concatenate(hots, axis=1), jnp.concatenate(parts, axis=0))

    def row_hot(line, height):
        line16 = jnp.broadcast_to(line, (16, LANES)).astype(jnp.int16)
        return jnp.concatenate(
            [hot(line16 == iota_c[k * 16 : k * 16 + 16, :]) for k in range(height // 16)], axis=0
        )

    def total_of(ref):
        total = ref[0].astype(F32)
        for i in range(1, 4):
            total = total + ref[i].astype(F32)
        return total.astype(BF16)

    w_s = ewi_ref[D : 2 * D]

    def send_border():
        for j in range(4):
            border[j * HALO : (j + 1) * HALO, :] = mm_t(
                f2[HALO : 2 * HALO, j * D : (j + 1) * D].astype(BF16), w_s
            ).astype(BF16)
            start(j)

    scatter(True, 0, 1)
    pl.semaphore_wait(barrier, peers + len(others))
    stage = [send(0, wg_ref.at[half_rows(1 - core), :], pair, partner)]
    started = list(stage)
    stage[0].start()
    scatter(True, 1, 2)
    stage[0].wait_recv()
    half[...] = (wg_ref[half_rows(core), :].astype(F32) + pair[...].astype(F32)).astype(BF16)
    stage = [
        send(i, half.at[quarter_rows(to), :], quarter.at[i], device)
        for i, (to, device) in enumerate(y_peers, 1)
    ]
    for c in stage:
        c.start()
    started += stage
    scatter(True, 2, 4)
    for c in stage:
        c.wait_recv()
    quarter[0] = half[quarter_rows(y), :]
    part[...] = total_of(quarter)
    stage = [send(i, part, along_z.at[z], device) for i, device in enumerate(z_peers, 4)]
    for c in stage:
        c.start()
    started += stage
    along_z[z] = part[...]
    scatter(True, 4, STEPS)
    send_border()
    for c in stage:
        c.wait_recv()
    other[...] = total_of(along_z)
    stage = [send(i, other, along_x.at[x], device) for i, device in enumerate(x_peers, 7)]
    for c in stage:
        c.start()
    started += stage
    along_x[x] = other[...]
    scatter(False, 0, 2)
    for c in stage:
        c.wait_recv()
    third[mine(), :] = total_of(along_x)
    stage = [
        send(i, third.at[mine(), :], third.at[mine(), :], device)
        for i, (_, device) in enumerate(y_peers, 10)
    ]
    for c in stage:
        c.start()
    started += stage
    scatter(False, 2, 4)

    for c in stage:
        c.wait_recv()
    stage = [send(13, third.at[half_rows(core), :], third.at[half_rows(core), :], partner)]
    stage[0].start()
    started += stage
    scatter(False, 4, STEPS)
    for j in range(4):
        rows = slice(j * HALO, (j + 1) * HALO)
        near = f2[0:HALO, j * D : (j + 1) * D].astype(BF16)
        node_ref[rows, :] = own_ref[rows, :] + mm_t(near, w_s)
    hots = [
        row_hot(out_rows_ref[j : j + 1, c * LANES : (c + 1) * LANES], NODES)
        for j in range(4)
        for c in range(HALO // LANES)
    ]
    for j in range(4):
        finish(j)
    node_ref[...] += mm(jnp.concatenate(hots, axis=1), landing[...])
    stage[0].wait_recv()
    sum_ref[...] = third[...]
    for c in started:
        c.wait_send()


def scatter_call(wide, narrow, first, send, own, wg, ewi, out_rows):
    vm = pl.BlockSpec(memory_space=pltpu.VMEM)
    v = pltpu.VMEM
    sem = pltpu.SemaphoreType.DMA
    quarter = W_ROWS // 8
    return pl.pallas_call(
        functools.partial(scatter_kernel, wide, narrow),
        out_shape=(
            jax.ShapeDtypeStruct((NODES, D), F32),
            jax.ShapeDtypeStruct((W_ROWS, D), BF16),
        ),
        in_specs=[pl.BlockSpec(memory_space=pl.ANY)] + [vm] * 5,
        out_specs=(vm, vm),
        scratch_shapes=[
            v((EDGES, D), BF16), v((2 * HALO, 4 * D), F32), v((NODES, LANES), jnp.int16),
            v((4 * HALO, D), BF16), v((4 * HALO, D), BF16),
            v((W_ROWS // 2, D), BF16), v((W_ROWS // 2, D), BF16), v((4, quarter, D), BF16),
            v((quarter, D), BF16), v((4, quarter, D), BF16), v((quarter, D), BF16),
            v((4, quarter, D), BF16), v((W_ROWS, D), BF16),
            sem((STEPS,)), sem((4,)), sem((4,)), sem((14,)), sem((14,)),
        ],
        compiler_params=pltpu.CompilerParams(
            collective_id=1, has_side_effects=True, vmem_limit_bytes=VMEM_LIMIT
        ),
        name="scatter",
    )(first, send, own, wg, ewi, out_rows)


def unpack_kernel(scales, node_ref, sum_ref, node_out, *rest):
    *outs, sem = rest
    copy = pltpu.make_async_copy(node_ref, node_out, sem)
    copy.start()
    at = 0
    for out, scale in zip(outs, scales):
        rows = out.shape[0]
        out[...] = sum_ref[at : at + rows, :].astype(F32) * scale
        at += rows
    copy.wait()


def unpack_call(scales, node, summed, shapes):
    vm = pl.BlockSpec(memory_space=pltpu.VMEM)
    hb = pl.BlockSpec(memory_space=pl.ANY)
    return pl.pallas_call(
        functools.partial(unpack_kernel, scales),
        out_shape=(jax.ShapeDtypeStruct((NODES, D), F32),)
        + tuple(jax.ShapeDtypeStruct(s, F32) for s in shapes),
        in_specs=[vm, vm],
        out_specs=(hb,) + (vm,) * 6,
        scratch_shapes=[pltpu.SemaphoreType.DMA(())],
        compiler_params=pltpu.CompilerParams(vmem_limit_bytes=VMEM_LIMIT),
        name="unpack",
    )(node, summed)


def per_device(
    wide,
    narrow,
    node_hidden_state,
    edge_hidden_state,
    node_output_gradient,
    edge_output_gradient,
    senders,
    receivers,
    edge_slot_count,
    outbound_rows,
    *weights,
):
    out_rows = outbound_rows.reshape(4, HALO)
    send = senders.reshape(EDGES // LANES, LANES)
    recv = receivers.reshape(EDGES // LANES, LANES)
    picked = gather_call(wide, narrow, node_hidden_state, out_rows, send)
    edge_grad, first, own, wg = partition_call(
        edge_slot_count,
        node_hidden_state,
        node_output_gradient,
        edge_hidden_state,
        edge_output_gradient,
        picked,
        recv,
        weights,
    )
    node_grad, summed = scatter_call(wide, narrow, first, send, own, wg, weights[0], out_rows)
    edge_scale = 1.0 / math.sqrt(EDGES * wide * narrow)
    node_scale = 1.0 / math.sqrt(NODES * wide * narrow)
    node_grad, *sums = unpack_call(
        (edge_scale,) * 3 + (node_scale,) * 3, node_grad, summed, [x.shape for x in weights]
    )
    return (node_grad, edge_grad, *sums)


def solution(mesh):
    both = ("wide", "narrow")
    rows, flat = P(both, None), P(both)
    return jax.shard_map(
        functools.partial(per_device, mesh.shape["wide"], mesh.shape["narrow"]),
        mesh=mesh,
        in_specs=(rows, rows, rows, rows, flat, flat, flat, P(both, None, None)) + (P(),) * 6,
        out_specs=(rows, rows) + (P(),) * 6,
        check_vma=False,
    )
```
